32 devices in a mesh: shot: 4 (over y, x), box: 8 (over z, core).
Axes of the slice: x: 2, y: 2, z: 4, core: 2. Of those that a mesh axis runs over, the one named last changes fastest.
Arguments:
- u_prev: float32 [4, 8, 128, 256], P('shot', None, 'box'), may hold values from -6 to 6
- u_now: float32 [4, 8, 128, 256], P('shot', None, 'box'), may hold values from -6 to 6
- born_prev: float32 [4, 8, 128, 256], P('shot', None, 'box'), may hold values from -6 to 6
- born_now: float32 [4, 8, 128, 256], P('shot', None, 'box'), may hold values from -6 to 6
- adj_after: float32 [4, 8, 128, 256], P('shot', None, 'box'), may hold values from -6 to 6
- adj_last: float32 [4, 8, 128, 256], P('shot', None, 'box'), may hold values from -6 to 6
- velocity: float32 [4, 128, 256], P('shot', 'box'), may hold values from 0.08 to 0.45
- wavelet: float32 [4, 8, 4], P('shot'), may hold values from -12 to 12
- sources: int32 [4, 8], P('shot'), may hold values from 0 to 32767
- receivers: int32 [4, 64], P('shot', 'box'), may hold values from 0 to 32575, as said below
- observed: float32 [4, 8, 4, 64], P('shot', None, None, 'box'), may hold values from -6 to 6
- first_tile: int32 [4], P('shot'), may hold values from 0 to 32
- reflectivity: float32 [12, 8, 2, 256], P(None, 'box'), may hold values from -6 to 6
Outputs:
- migrated: float32 [12, 8, 2, 256], P(None, 'box')
The draws below stay inside these ranges and needn't reach their ends.
Inputs may be any that keep to these rules, and one draw needn't show every extreme that they name: `receivers`: receiver r of every group lies in the grid columns r * 2 to (r + 1) * 2 - 1 of its box, at a depth cell under 256 // 4.
All inputs are finite; a program needn't handle non-finite values.
Results may differ from the reference program's by a relative error of at most 0.00011.
Values sent between devices are 32-bit elements; how exact they have to be, the bound alone decides.
No kernel may reach another device: no remote copies, remote signals or barrier semaphores. Data moves between devices by JAX's collectives and lax.ppermute only.
A program may use at most 64 MiB of HBM per device.

```python
import math
import jax
import jax.numpy as jnp
from jax import lax

NS = 8
NZ = 256
TW = 2
STEPS = 4
GROUPS = 4
OWNERS = 8
ROUNDS = 12
NXB = 128
NREC = 64
N_BOX = 8


def draw_receivers(key, part):
    key_column, key_depth = jax.random.split(key)
    jitter = jax.random.randint(key_column, (GROUPS, NREC), 0, TW, dtype=jnp.int32)
    depth_cell = jax.random.randint(key_depth, (GROUPS, NREC), 0, NZ // 4, dtype=jnp.int32)
    jitter = jitter.at[:, 0].set(0).at[:, NREC - 1].set(TW - 1)
    depth_cell = depth_cell.at[:, 0].set(0).at[:, NREC - 1].set(NZ // 4 - 1)
    column = jnp.arange(NREC, dtype=jnp.int32)[None, :] * TW + jitter
    return column * NZ + depth_cell


def set_ends(drawn, stream_key, smallest, top_value):
    spot = [jax.random.randint(jax.random.fold_in(stream_key, axis), (), 0, length) for axis, length in enumerate(drawn.shape)]
    longest = drawn.shape.index(max(drawn.shape))
    beside = spot[:longest] + [(spot[longest] + 1) % drawn.shape[longest]] + spot[longest + 1:]
    return drawn.at[tuple(spot)].set(smallest).at[tuple(beside)].set(top_value)


def block_levels(own_key, dims, cuts, least, largest):
    loudness, own = 1.0, jax.random.fold_in(own_key, 6)
    for dim, blocks in cuts:
        draws = jnp.exp(jax.random.uniform(jax.random.fold_in(own, dim), (blocks,), jnp.float32, least / len(cuts), largest / len(cuts)))
        loudness = loudness * jnp.repeat(draws, dims[dim] // blocks).reshape([-1 if axis == dim else 1 for axis in range(len(dims))])
    return loudness


def noise(key, dims, spread, bound, shards=(), kind=jnp.bfloat16):
    array = spread * jax.random.normal(key, dims, jnp.float32)
    if shards:
        array = array * block_levels(key, dims, shards, -0.22, 0.18)
    return jnp.clip(array, -bound, bound).astype(kind)


def setup_inputs(seed: int = 0) -> dict:
    seeds = jax.random.split(jax.random.key(seed), 14)
    u_prev = noise(seeds[0], (GROUPS, NS, NXB, NZ), 1.0, 6.0, ((0, 4), (2, 8)), jnp.float32)
    u_now = noise(seeds[1], (GROUPS, NS, NXB, NZ), 1.0, 6.0, ((0, 4), (2, 8)), jnp.float32)
    born_prev = noise(seeds[2], (GROUPS, NS, NXB, NZ), 1.0, 6.0, ((0, 4), (2, 8)), jnp.float32)
    born_now = noise(seeds[3], (GROUPS, NS, NXB, NZ), 1.0, 6.0, ((0, 4), (2, 8)), jnp.float32)
    adj_after = noise(seeds[4], (GROUPS, NS, NXB, NZ), 1.0, 6.0, ((0, 4), (2, 8)), jnp.float32)
    adj_last = noise(seeds[5], (GROUPS, NS, NXB, NZ), 1.0, 6.0, ((0, 4), (2, 8)), jnp.float32)
    velocity = jnp.clip(jnp.exp(math.log(0.45) - 1.7272209 * jax.random.uniform(seeds[6], (GROUPS, NXB, NZ), jnp.float32) ** block_levels(seeds[6], (GROUPS, NXB, NZ), ((0, 4), (1, 8)), -0.2, 0.2)), 0.08, 0.45)
    wavelet = noise(seeds[7], (GROUPS, NS, STEPS), 3.0, 12.0, ((0, 4),), jnp.float32)
    sources = set_ends(jax.random.randint(seeds[8], (GROUPS, NS), 0, NXB * NZ), jax.random.fold_in(seeds[8], 1), 0, (NXB * NZ) - 1).astype(jnp.int32)
    receivers = draw_receivers(jax.random.fold_in(seeds[13], 71), 0)
    observed = noise(seeds[10], (GROUPS, NS, STEPS, NREC), 1.0, 6.0, ((0, 4), (3, 8)), jnp.float32)
    first_tile = set_ends(jax.random.randint(seeds[11], (GROUPS,), 0, (ROUNDS - N_BOX) * N_BOX + 1), jax.random.fold_in(seeds[11], 1), 0, (ROUNDS - N_BOX) * N_BOX).astype(jnp.int32)
    reflectivity = noise(seeds[12], (ROUNDS, OWNERS, TW, NZ), 1.0, 6.0, ((1, 8),), jnp.float32)
    return {"u_prev": u_prev, "u_now": u_now, "born_prev": born_prev, "born_now": born_now, "adj_after": adj_after, "adj_last": adj_last, "velocity": velocity, "wavelet": wavelet, "sources": sources, "receivers": receivers, "observed": observed, "first_tile": first_tile, "reflectivity": reflectivity}


damping = 1.0

def laplace(wavefield):
    padded = jnp.pad(wavefield, ((0, 0), (1, 1), (1, 1)))
    return padded[:, 2:, 1:-1] + padded[:, :-2, 1:-1] + padded[:, 1:-1, 2:] + padded[:, 1:-1, :-2] - 4.0 * wavefield

def add_sources(wavefield, cells, amount):
    flat = wavefield.reshape(wavefield.shape[0], -1)
    lanes = jnp.arange(wavefield.shape[0], dtype=jnp.int32)
    return flat.at[lanes, cells].add(amount).reshape(wavefield.shape)

def add_receivers(wavefield, cells, amount):
    flat = wavefield.reshape(wavefield.shape[0], -1)
    return flat.at[:, cells].add(amount).reshape(wavefield.shape)

def read_receivers(wavefield, cells):
    flat = wavefield.reshape(wavefield.shape[0], -1)
    return flat[:, cells]

def reference(u_prev, u_now, born_prev, born_now, adj_after, adj_last, velocity, wavelet, sources, receivers, observed, first_tile, reflectivity):
    image_flat = reflectivity.reshape(ROUNDS * OWNERS * TW, NZ)
    gradient = jnp.zeros_like(image_flat)
    illumination = jnp.zeros_like(image_flat)
    for group in range(GROUPS):
        speed = velocity[group]
        first_column = (first_tile[group] * TW).astype(jnp.int32)
        image_box = lax.dynamic_slice_in_dim(image_flat, first_column, NXB, 0)
        older_u, newer_u = (u_prev[group], u_now[group])
        older_b, newer_b = (born_prev[group], born_now[group])
        accelerations = []
        misfits = []
        for moment in range(STEPS):
            next_u = 2.0 * newer_u - older_u + speed * laplace(newer_u)
            next_u = add_sources(next_u, sources[group], wavelet[group, :, moment])
            second_diff = next_u - 2.0 * newer_u + older_u
            next_b = 2.0 * newer_b - older_b + speed * laplace(newer_b) + image_box * second_diff
            accelerations.append(second_diff)
            misfits.append(read_receivers(next_b, receivers[group]) - observed[group, :, moment, :])
            older_u, newer_u = (newer_u, next_u)
            older_b, newer_b = (newer_b, next_b)
        adjoint_old, adjoint_new = (adj_after[group], adj_last[group])
        grad_box = jnp.zeros((NXB, NZ), jnp.float32)
        illum_box = jnp.zeros((NXB, NZ), jnp.float32)
        for moment in reversed(range(STEPS)):
            adjoint_next = 2.0 * adjoint_new - adjoint_old + speed * laplace(adjoint_new)
            adjoint_next = add_receivers(adjoint_next, receivers[group], misfits[moment])
            grad_box = grad_box + lax.optimization_barrier(jnp.sum(adjoint_next * accelerations[moment], axis=0))
            illum_box = illum_box + lax.optimization_barrier(jnp.sum(accelerations[moment] * accelerations[moment], axis=0))
            adjoint_old, adjoint_new = (adjoint_new, adjoint_next)
        old_grad = lax.dynamic_slice_in_dim(gradient, first_column, NXB, 0)
        gradient = lax.dynamic_update_slice_in_dim(gradient, old_grad + grad_box, first_column, 0)
        old_illum = lax.dynamic_slice_in_dim(illumination, first_column, NXB, 0)
        illumination = lax.dynamic_update_slice_in_dim(illumination, old_illum + illum_box, first_column, 0)
    migrated = gradient / jnp.sqrt(illumination + damping)
    return migrated.reshape(ROUNDS, OWNERS, TW, NZ)
```

```python
import functools

import jax
import jax.numpy as jnp
from jax import lax
from jax.experimental import pallas as pl
from jax.experimental.pallas import tpu as pltpu
from jax.sharding import PartitionSpec as P

damping = 1.0
LANES = 128
MARGIN = 8
STEPS = 4
HALO = (
    ("un", 0, 7),
    ("up", 0, 6),
    ("bn", 0, 7),
    ("bp", 0, 6),
    ("un", 1, 4),
    ("up", 1, 3),
    ("qn", 0, 4),
    ("qn", 1, 4),
    ("qp", 0, 3),
    ("qp", 1, 3),
)
HALO_TILES = sum(count for _, _, count in HALO)
SPEED_TILE = HALO_TILES
META_TILE = HALO_TILES + 2
PACK_TILES = HALO_TILES + 3
VMEM = pltpu.VMEM
SMEM = pltpu.SMEM


def lane_iota():
    return lax.broadcasted_iota(jnp.int32, (8, LANES), 1)


def pack_kernel(
    first, rec, un, up, bn, bp, qn, qp, speed, obs, refl, pack_a, pack_b, image_out, *, owners
):
    columns, depth = speed.shape[1], speed.shape[2]
    rounds = refl.shape[0]
    tiles = columns // 2
    position = lax.axis_index("box")
    even = lax.rem(position, 2) == 0
    refs = {"un": un, "up": up, "bn": bn, "bp": bp, "qn": qn, "qp": qp}

    for target in range(owners):
        low_tile = first[0] + tiles * target - 3
        r0 = lax.div(low_tile - position + 2 * owners - 1, owners) - 1
        for slot in range(2):
            r = jnp.clip(r0 + slot, 0, rounds - 1)
            image_out[target, 2 * slot : 2 * slot + 2, :] = refl[r, 0, :, 0:LANES]

    def put(tile, left, right):
        pack_a[tile] = jnp.where(even, right, left)
        pack_b[tile] = jnp.where(even, left, right)

    tile = 0
    for name, half, count in HALO:
        part = slice(half * LANES, (half + 1) * LANES)
        low = jnp.swapaxes(refs[name][0, :, 0:8, part], 0, 1)
        high = jnp.swapaxes(refs[name][0, :, columns - 8 : columns, part], 0, 1)
        for j in range(1, count + 1):
            put(tile, low[j - 1], high[8 - j])
            tile += 1
    for half in range(2):
        part = slice(half * LANES, (half + 1) * LANES)
        put(SPEED_TILE + half, speed[0, 0:8, part], speed[0, columns - 8 : columns, part])

    lane = lane_iota()
    count = rec.shape[1]

    def meta(right):
        out = jnp.zeros((8, LANES), jnp.float32)
        for k in range(2):
            r = count - 1 - k if right else k
            for t in range(STEPS):
                value = jnp.broadcast_to(obs[0, :, t, r : r + 1], (8, LANES))
                out = jnp.where(lane == 2 * t + k, value, out)
            column = lax.div(rec[0, r], depth) - position * columns
            distance = columns - column if right else column + 1
            code = distance * depth + lax.rem(rec[0, r], depth)
            out = jnp.where(lane == 2 * STEPS + k, code.astype(jnp.float32), out)
        return out

    put(META_TILE, meta(False), meta(True))


def wave_kernel(
    first,
    sources,
    rec,
    un,
    up,
    bn,
    bp,
    qn,
    qp,
    speed,
    obs,
    wavelet,
    pack_a,
    pack_b,
    image_in,
    out,
    u0,
    u1,
    b0,
    b1,
    q0,
    q1,
    vel,
    img,
    acc,
    *,
    owners,
    groups,
):
    columns, depth = speed.shape[1], speed.shape[2]
    tiles = columns // 2
    position = lax.axis_index("box")
    even = lax.rem(position, 2) == 0
    lane = lane_iota()
    first_lane = lane == 0
    last_lane = lane == LANES - 1
    zero = jnp.zeros((8, LANES), jnp.float32)
    halves = (slice(0, LANES), slice(LANES, 2 * LANES))
    scratch = {"un": u0, "up": u1, "bn": b0, "bp": b1, "qn": q0, "qp": q1}

    for name, ref in (("un", un), ("up", up), ("qn", qn), ("qp", qp)):
        for c in range(0, columns, 8):
            scratch[name][MARGIN + c : MARGIN + c + 8] = jnp.swapaxes(ref[0, :, c : c + 8, :], 0, 1)
    for name, ref in (("bn", bn), ("bp", bp)):
        for c in range(0, columns, 8):
            scratch[name][MARGIN + c : MARGIN + c + 8] = jnp.swapaxes(
                ref[0, :, c : c + 8, 0:LANES], 0, 1
            )
    for c in range(columns):
        vel[MARGIN + c] = jnp.broadcast_to(speed[0, c : c + 1, :], (8, depth))

    def got(tile):
        a, b = pack_a[tile], pack_b[tile]
        return jnp.where(even, b, a), jnp.where(even, a, b)

    tile = 0
    for name, half, count in HALO:
        for j in range(1, count + 1):
            left, right = got(tile)
            scratch[name][MARGIN - j, :, halves[half]] = left
            scratch[name][MARGIN + columns - 1 + j, :, halves[half]] = right
            tile += 1
    for half, count in ((0, 6), (1, 3)):
        left, right = got(SPEED_TILE + half)
        for j in range(1, count + 1):
            vel[MARGIN - j, :, halves[half]] = jnp.broadcast_to(left[8 - j : 9 - j], (8, LANES))
            vel[MARGIN + columns - 1 + j, :, halves[half]] = jnp.broadcast_to(
                right[j - 1 : j], (8, LANES)
            )
    meta_left, meta_right = got(META_TILE)

    low_tile = first[0] + tiles * position - 3 + owners
    for m in range(tiles + 6):
        owner = lax.rem(low_tile + m, owners)
        pair = image_in[owner, 2 * (m // owners) : 2 * (m // owners) + 2, :]
        for w in range(2):
            img[MARGIN - 6 + 2 * m + w] = jnp.broadcast_to(pair[w : w + 1], (8, LANES))

    shot = lax.broadcasted_iota(jnp.int32, (8, LANES), 0)
    cell = jnp.zeros((8, LANES), jnp.int32)
    for s in range(8):
        cell = jnp.where(shot == s, sources[0, s] - position * columns * depth, cell)
    cell = cell - lane
    pulses = [jnp.broadcast_to(wavelet[0, :, t : t + 1], (8, LANES)) for t in range(STEPS)]

    def receiver(c):
        if c < 0 or c >= columns:
            j = -c if c < 0 else c - columns + 1
            meta = meta_left if c < 0 else meta_right
            k = (j - 1) // 2
            lane_of = 2 * STEPS + k
            code = jnp.broadcast_to(meta[:, lane_of : lane_of + 1], (8, LANES))
            mask = code == (lane + j * depth).astype(jnp.float32)
            return mask, lambda t: jnp.broadcast_to(
                meta[:, 2 * t + k : 2 * t + k + 1], (8, LANES)
            )
        r = c // 2
        here = rec[0, r] - (position * columns + c) * depth
        mask = lane == here
        return mask, lambda t: jnp.broadcast_to(obs[0, :, t, r : r + 1], (8, LANES))

    def up_down(xs):
        rolled_up = [pltpu.roll(x, 1, 1) for x in xs]
        rolled_down = [pltpu.roll(x, LANES - 1, 1) for x in xs]
        if len(xs) == 1:
            return [jnp.where(first_lane, 0.0, rolled_up[0]) + rolled_down[0]]
        return [
            jnp.where(first_lane, 0.0, rolled_up[0])
            + jnp.where(last_lane, rolled_down[1], rolled_down[0]),
            jnp.where(first_lane, rolled_up[0], rolled_up[1])
            + jnp.where(last_lane, 0.0, rolled_down[1]),
        ]

    def lap(ref, e, count):
        mid = [ref[e, :, halves[h]] for h in range(count)]
        depthwise = up_down(mid)
        return mid, [
            ref[e - 1, :, halves[h]] + ref[e + 1, :, halves[h]] + depthwise[h] - 4.0 * mid[h]
            for h in range(count)
        ]

    new_u, old_u, new_b, old_b = u0, u1, b0, b1
    misfits = []
    for t in range(STEPS):
        wide, narrow = 6 - t, 3 - t
        for c in range(-wide, columns + wide):
            e = MARGIN + c
            count = 2 if -narrow <= c < columns + narrow else 1
            mid, laps = lap(new_u, e, count)
            for h in range(count):
                hit = cell == c * depth + h * LANES
                a = vel[e, :, halves[h]] * laps[h] + jnp.where(hit, pulses[t], 0.0)
                acc[t, e, :, halves[h]] = a
                old_u[e, :, halves[h]] = 2.0 * mid[h] - old_u[e, :, halves[h]] + a
            (mid_b,), (lap_b,) = lap(new_b, e, 1)
            old_b[e] = (
                2.0 * mid_b
                - old_b[e]
                + vel[e, :, halves[0]] * lap_b
                + img[e] * acc[t, e, :, halves[0]]
            )
        new_u, old_u = old_u, new_u
        new_b, old_b = old_b, new_b
        part = {}
        for c in range(-t, columns + t):
            mask, recorded = receiver(c)
            part[c] = jnp.where(mask, new_b[MARGIN + c] - recorded(t), 0.0)
        misfits.append(part)

    grad = [[zero, zero] for _ in range(columns)]
    new_q, old_q = q0, q1
    for t in reversed(range(STEPS)):
        for c in range(-t, columns + t):
            e = MARGIN + c
            mid, laps = lap(new_q, e, 2)
            for h in range(2):
                q = 2.0 * mid[h] - old_q[e, :, halves[h]] + vel[e, :, halves[h]] * laps[h]
                if h == 0:
                    q = q + misfits[t][c]
                old_q[e, :, halves[h]] = q
                if 0 <= c < columns:
                    grad[c][h] = grad[c][h] + q * acc[t, e, :, halves[h]]
        new_q, old_q = old_q, new_q

    start = jnp.full((1, LANES), first[0].astype(jnp.float32))
    for k in range(tiles):
        owner = lax.rem(first[0] + tiles * position + k, owners)
        rows = []
        for h in range(2):
            for w in range(2):
                rows.append(jnp.sum(grad[2 * k + w][h], axis=0, keepdims=True))
        for h in range(2):
            for w in range(2):
                e = MARGIN + 2 * k + w
                total = zero
                for t in range(STEPS):
                    a = acc[t, e, :, halves[h]]
                    total = total + a * a
                rows.append(jnp.sum(total, axis=0, keepdims=True))
        for group in range(groups):
            for i, row in enumerate(rows):
                out[group * owners + owner, :, i * LANES : (i + 1) * LANES] = row
            out[group * owners + owner, :, 8 * LANES : 9 * LANES] = start


def join_kernel(received, migrated, total, *, owners, groups):
    position = lax.axis_index("box")
    total[...] = jnp.zeros_like(total)
    for group in range(groups):
        start = received[group * owners, 0, 8 * LANES].astype(jnp.int32)
        base = lax.div(start - position + owners - 1, owners)
        for p in range(owners):
            total[base + p] = total[base + p] + received[group * owners + p, :, 0 : 8 * LANES]
    for r in range(migrated.shape[0]):
        grad = total[r, :, 0 : 4 * LANES]
        illum = total[r, :, 4 * LANES : 8 * LANES]
        image = grad / jnp.sqrt(illum + damping)
        for h in range(2):
            for w in range(2):
                i = 2 * h + w
                migrated[r, 0, w : w + 1, h * LANES : (h + 1) * LANES] = image[
                    :, i * LANES : (i + 1) * LANES
                ]


def on_device(
    u_prev,
    u_now,
    born_prev,
    born_now,
    adj_after,
    adj_last,
    velocity,
    wavelet,
    sources,
    receivers,
    observed,
    first_tile,
    reflectivity,
):
    owners = lax.axis_size("box")
    groups = lax.axis_size("shot")
    columns, depth = velocity.shape[1], velocity.shape[2]
    rounds = reflectivity.shape[0]
    smem, vmem = pl.BlockSpec(memory_space=SMEM), pl.BlockSpec(memory_space=VMEM)
    f32 = jnp.float32
    params = pltpu.CompilerParams(vmem_limit_bytes=48 * 1024 * 1024)
    fields = (u_now, u_prev, born_now, born_prev, adj_last, adj_after)

    pack = jax.ShapeDtypeStruct((PACK_TILES, 8, LANES), f32)
    send_a, send_b, image_out = pl.pallas_call(
        functools.partial(pack_kernel, owners=owners),
        out_shape=(pack, pack, jax.ShapeDtypeStruct((owners, 4, LANES), f32)),
        in_specs=[smem] * 2 + [vmem] * 9,
        out_specs=(vmem,) * 3,
        compiler_params=params,
        name="pack",
    )(first_tile, receivers, *fields, velocity, observed, reflectivity)

    image_in = lax.all_to_all(image_out, "box", split_axis=0, concat_axis=0, tiled=True)
    swap_a = [(i, i ^ 1) for i in range(owners)]
    swap_b = [(i, i + 1 if i % 2 else i - 1) for i in range(1, owners - 1)]
    got_a = lax.ppermute(send_a, "box", swap_a)
    got_b = lax.ppermute(send_b, "box", swap_b)

    ext = columns + 2 * MARGIN
    out = pl.pallas_call(
        functools.partial(wave_kernel, owners=owners, groups=groups),
        out_shape=jax.ShapeDtypeStruct((groups * owners, 1, 9 * LANES), f32),
        in_specs=[smem] * 3 + [vmem] * 12,
        out_specs=vmem,
        scratch_shapes=[
            VMEM((ext, 8, depth), f32),
            VMEM((ext, 8, depth), f32),
            VMEM((ext, 8, LANES), f32),
            VMEM((ext, 8, LANES), f32),
            VMEM((ext, 8, depth), f32),
            VMEM((ext, 8, depth), f32),
            VMEM((ext, 8, depth), f32),
            VMEM((ext, 8, LANES), f32),
            VMEM((STEPS, ext, 8, depth), f32),
        ],
        compiler_params=params,
        name="waves",
    )(
        first_tile,
        sources,
        receivers,
        *fields,
        velocity,
        observed,
        wavelet,
        got_a,
        got_b,
        image_in,
    )

    received = lax.all_to_all(out, ("shot", "box"), split_axis=0, concat_axis=0, tiled=True)
    return pl.pallas_call(
        functools.partial(join_kernel, owners=owners, groups=groups),
        out_shape=jax.ShapeDtypeStruct(reflectivity.shape, f32),
        in_specs=[vmem],
        out_specs=vmem,
        scratch_shapes=[VMEM((rounds, 1, 8 * LANES), f32)],
        compiler_params=params,
        name="join",
    )(received)


def solution(mesh):
    return jax.shard_map(
        on_device,
        mesh=mesh,
        in_specs=(
            P("shot", None, "box", None),
            P("shot", None, "box", None),
            P("shot", None, "box", None),
            P("shot", None, "box", None),
            P("shot", None, "box", None),
            P("shot", None, "box", None),
            P("shot", "box", None),
            P("shot", None, None),
            P("shot", None),
            P("shot", "box"),
            P("shot", None, None, "box"),
            P("shot"),
            P(None, "box", None, None),
        ),
        out_specs=P(None, "box", None, None),
        check_vma=False,
    )
```

```python
import functools

import jax
import jax.numpy as jnp
from jax import lax
from jax.experimental import pallas as pl
from jax.experimental.pallas import tpu as pltpu
from jax.sharding import PartitionSpec as P

damping = 1.0
LANES = 128
MARGIN = 8
STEPS = 4
HALO = (
    ("un", 0, 7),
    ("up", 0, 6),
    ("bn", 0, 7),
    ("bp", 0, 6),
    ("un", 1, 4),
    ("up", 1, 3),
    ("qn", 0, 4),
    ("qn", 1, 4),
    ("qp", 0, 3),
    ("qp", 1, 3),
)
HALO_TILES = sum(count for _, _, count in HALO)
SPEED_TILE = HALO_TILES
META_TILE = HALO_TILES + 2
PACK_TILES = HALO_TILES + 3
VMEM = pltpu.VMEM
SMEM = pltpu.SMEM


def lane_iota():
    return lax.broadcasted_iota(jnp.int32, (8, LANES), 1)


def pack_kernel(
    first_any,
    rec_any,
    un,
    up,
    bn,
    bp,
    qn,
    qp,
    speed_any,
    obs_any,
    refl_any,
    pack_a,
    pack_b,
    image_out,
    first,
    rec,
    refl,
    wide,
    near,
    speed,
    obs,
    sems,
):
    columns, depth = un.shape[2], un.shape[3]
    position = lax.axis_index("box")
    even = lax.rem(position, 2) == 0
    edges = (pl.ds(0, 8), pl.ds(columns - 8, 8))
    wides = {"un": 0, "up": 1, "qn": 2, "qp": 3}
    nears = {"bn": 0, "bp": 1}
    moves = [(first_any, first), (rec_any, rec), (obs_any, obs), (refl_any, refl)]
    for side in range(2):
        for name, ref in (("un", un), ("up", up), ("qn", qn), ("qp", qp)):
            moves.append((ref.at[0, :, edges[side], :], wide.at[side, wides[name]]))
        for name, ref in (("bn", bn), ("bp", bp)):
            moves.append((ref.at[0, :, edges[side], pl.ds(0, LANES)], near.at[side, nears[name]]))
        moves.append((speed_any.at[0, edges[side], :], speed.at[side]))
    copies = [pltpu.make_async_copy(*move, sems.at[i]) for i, move in enumerate(moves)]
    for copy in copies:
        copy.start()
    for copy in copies:
        copy.wait()

    owners = image_out.shape[0]
    for target in range(owners):
        low_tile = first[0] + (columns // 2) * target - 3
        r0 = lax.div(low_tile - position + 2 * owners - 1, owners) - 1
        for slot in range(2):
            r = jnp.clip(r0 + slot, 0, refl.shape[0] - 1)
            image_out[target, 2 * slot : 2 * slot + 2, :] = refl[r, 0, :, 0:LANES]

    def put(tile, left, right):
        pack_a[tile] = jnp.where(even, right, left)
        pack_b[tile] = jnp.where(even, left, right)

    tile = 0
    for name, half, count in HALO:
        part = slice(half * LANES, (half + 1) * LANES)
        if name in nears:
            low, high = (near[side, nears[name]] for side in range(2))
        else:
            low, high = (wide[side, wides[name], :, :, part] for side in range(2))
        low, high = jnp.swapaxes(low, 0, 1), jnp.swapaxes(high, 0, 1)
        for j in range(1, count + 1):
            put(tile, low[j - 1], high[8 - j])
            tile += 1
    for half in range(2):
        part = slice(half * LANES, (half + 1) * LANES)
        put(SPEED_TILE + half, speed[0, :, part], speed[1, :, part])

    lane = lane_iota()
    count = rec.shape[1]

    def meta(right):
        out = jnp.zeros((8, LANES), jnp.float32)
        for k in range(2):
            r = count - 1 - k if right else k
            for t in range(STEPS):
                value = jnp.broadcast_to(obs[0, :, t, r : r + 1], (8, LANES))
                out = jnp.where(lane == 2 * t + k, value, out)
            column = lax.div(rec[0, r], depth) - position * columns
            distance = columns - column if right else column + 1
            code = distance * depth + lax.rem(rec[0, r], depth)
            out = jnp.where(lane == 2 * STEPS + k, code.astype(jnp.float32), out)
        return out

    put(META_TILE, meta(False), meta(True))


def depthwise(xs, first_lane, last_lane):
    rolled_up = [pltpu.roll(x, 1, 1) for x in xs]
    rolled_down = [pltpu.roll(x, LANES - 1, 1) for x in xs]
    if len(xs) == 1:
        return [
            jnp.where(first_lane, 0.0, rolled_up[0]) + jnp.where(last_lane, 0.0, rolled_down[0])
        ]
    return [
        jnp.where(first_lane, 0.0, rolled_up[0])
        + jnp.where(last_lane, rolled_down[1], rolled_down[0]),
        jnp.where(first_lane, rolled_up[0], rolled_up[1])
        + jnp.where(last_lane, 0.0, rolled_down[1]),
    ]


def lap(ref, e, count, edges):
    parts = [slice(h * LANES, (h + 1) * LANES) for h in range(count)]
    mid = [ref[e, :, part] for part in parts]
    along = depthwise(mid, *edges)
    return mid, [
        ref[e - 1, :, parts[h]] + ref[e + 1, :, parts[h]] + along[h] - 4.0 * mid[h]
        for h in range(count)
    ]


def homogeneous_kernel(
    sources,
    un,
    up,
    bn,
    bp,
    qn,
    qp,
    speed,
    wavelet,
    pack_a,
    pack_b,
    acc,
    b0,
    b1,
    near_speed,
    meta,
    rows_out,
    u0,
    u1,
    q0,
    q1,
    vel,
    late,
):
    columns, depth = speed.shape[1], speed.shape[2]
    position = lax.axis_index("box")
    even = lax.rem(position, 2) == 0
    has_left = position > 0
    has_right = position < lax.axis_size("box") - 1
    lane = lane_iota()
    edges = lane == 0, lane == LANES - 1
    zero = jnp.zeros((8, LANES), jnp.float32)
    halves = (slice(0, LANES), slice(LANES, 2 * LANES))
    scratch = {"un": u0, "up": u1, "bn": b0, "bp": b1, "qn": q0, "qp": q1}

    for name, ref in (("un", un), ("up", up), ("qn", qn), ("qp", qp)):
        for c in range(0, columns, 8):
            scratch[name][MARGIN + c : MARGIN + c + 8] = jnp.swapaxes(ref[0, :, c : c + 8, :], 0, 1)
    for name, ref in (("bn", bn), ("bp", bp)):
        for c in range(0, columns, 8):
            scratch[name][MARGIN + c : MARGIN + c + 8] = jnp.swapaxes(
                ref[0, :, c : c + 8, 0:LANES], 0, 1
            )
    for c in range(columns):
        vel[MARGIN + c] = jnp.broadcast_to(speed[0, c : c + 1, :], (8, depth))

    def got(tile):
        a, b = pack_a[tile], pack_b[tile]
        left, right = jnp.where(even, b, a), jnp.where(even, a, b)
        return jnp.where(has_left, left, 0.0), jnp.where(has_right, right, 0.0)

    tile = 0
    for name, half, count in HALO:
        for j in range(1, count + 1):
            left, right = got(tile)
            scratch[name][MARGIN - j, :, halves[half]] = left
            scratch[name][MARGIN + columns - 1 + j, :, halves[half]] = right
            tile += 1
    for half, count in ((0, 6), (1, 3)):
        left, right = got(SPEED_TILE + half)
        for j in range(1, count + 1):
            vel[MARGIN - j, :, halves[half]] = jnp.broadcast_to(left[8 - j : 9 - j], (8, LANES))
            vel[MARGIN + columns - 1 + j, :, halves[half]] = jnp.broadcast_to(
                right[j - 1 : j], (8, LANES)
            )
    meta_left, meta_right = got(META_TILE)
    meta[0] = meta_left
    meta[1] = meta_right
    for c in range(-6, columns + 6):
        near_speed[MARGIN + c] = vel[MARGIN + c, :, halves[0]]

    shot = lax.broadcasted_iota(jnp.int32, (8, LANES), 0)
    cell = jnp.zeros((8, LANES), jnp.int32)
    for s in range(8):
        cell = jnp.where(shot == s, sources[0, s] - position * columns * depth, cell)
    cell = cell - lane
    pulses = [jnp.broadcast_to(wavelet[0, :, t : t + 1], (8, LANES)) for t in range(STEPS)]

    new_u, old_u = u0, u1
    illum = [[zero, zero] for _ in range(columns)]
    for t in range(STEPS):
        wide, narrow = 6 - t, 3 - t
        for c in range(-wide, columns + wide):
            e = MARGIN + c
            count = 2 if -narrow <= c < columns + narrow else 1
            mid, laps = lap(new_u, e, count, edges)
            for h in range(count):
                hit = cell == c * depth + h * LANES
                a = vel[e, :, halves[h]] * laps[h] + jnp.where(hit, pulses[t], 0.0)
                if h == 0:
                    acc[t, e] = a
                elif 0 <= c < columns:
                    late[t, c] = a
                old_u[e, :, halves[h]] = 2.0 * mid[h] - old_u[e, :, halves[h]] + a
                if 0 <= c < columns:
                    illum[c][h] = illum[c][h] + a * a
        new_u, old_u = old_u, new_u

    grad = [[zero, zero] for _ in range(columns)]
    new_q, old_q = q0, q1
    for t in reversed(range(STEPS)):
        for c in range(-t, columns + t):
            e = MARGIN + c
            mid, laps = lap(new_q, e, 2, edges)
            for h in range(2):
                q = 2.0 * mid[h] - old_q[e, :, halves[h]] + vel[e, :, halves[h]] * laps[h]
                old_q[e, :, halves[h]] = q
                if 0 <= c < columns:
                    a = late[t, c] if h else acc[t, e]
                    grad[c][h] = grad[c][h] + q * a
        new_q, old_q = old_q, new_q

    for k in range(columns // 2):
        i = 0
        for sums in (grad, illum):
            for h in range(2):
                for w in range(2):
                    rows_out[k, :, i * LANES : (i + 1) * LANES] = jnp.sum(
                        sums[2 * k + w][h], axis=0, keepdims=True
                    )
                    i += 1


def scattered_kernel(
    first,
    rec,
    acc,
    b0_in,
    b1_in,
    speed,
    meta,
    rows_in,
    obs,
    image_in,
    out,
    b0,
    b1,
    q0,
    q1,
    img,
    *,
    owners,
    groups,
    depth,
):
    columns = 2 * rows_in.shape[0]
    tiles = columns // 2
    position = lax.axis_index("box")
    lane = lane_iota()
    edges = lane == 0, lane == LANES - 1
    zero = jnp.zeros((8, LANES), jnp.float32)

    low_tile = first[0] + tiles * position - 3 + owners
    for m in range(tiles + 6):
        owner = lax.rem(low_tile + m, owners)
        slot = 2 * (m // owners)
        pair = image_in[owner, slot : slot + 2, :]
        for w in range(2):
            img[MARGIN - 6 + 2 * m + w] = jnp.broadcast_to(pair[w : w + 1], (8, LANES))

    def receiver(c):
        if c < 0 or c >= columns:
            j = -c if c < 0 else c - columns + 1
            side = meta[0] if c < 0 else meta[1]
            k = (j - 1) // 2
            lane_of = 2 * STEPS + k
            code = jnp.broadcast_to(side[:, lane_of : lane_of + 1], (8, LANES))
            mask = code == (lane + j * depth).astype(jnp.float32)
            return mask, lambda t: jnp.broadcast_to(
                side[:, 2 * t + k : 2 * t + k + 1], (8, LANES)
            )
        r = c // 2
        here = rec[0, r] - (position * columns + c) * depth
        return lane == here, lambda t: jnp.broadcast_to(obs[0, :, t, r : r + 1], (8, LANES))

    misfits = []
    new_b, old_b, spare = b0_in, b1_in, [b0, b1]
    for t in range(STEPS):
        next_b = spare[t % 2]
        for c in range(t - 6, columns + 6 - t):
            e = MARGIN + c
            (mid,), (laps,) = lap(new_b, e, 1, edges)
            next_b[e] = 2.0 * mid - old_b[e] + speed[e] * laps + img[e] * acc[t, e]
        old_b, new_b = new_b, next_b
        part = {}
        for c in range(-t, columns + t):
            mask, recorded = receiver(c)
            part[c] = jnp.where(mask, new_b[MARGIN + c] - recorded(t), 0.0)
        misfits.append(part)

    grad = [zero] * columns
    new_q, old_q = q0, q1
    for t in reversed(range(STEPS)):
        for c in range(-t, columns + t):
            e = MARGIN + c
            q = misfits[t][c]
            if t < STEPS - 1:
                (mid,), (laps,) = lap(new_q, e, 1, edges)
                q = q + 2.0 * mid + speed[e] * laps
            if t < STEPS - 2:
                q = q - old_q[e]
            old_q[e] = q
            if 0 <= c < columns:
                grad[c] = grad[c] + q * acc[t, e]
        new_q, old_q = old_q, new_q

    start = jnp.full((1, LANES), first[0].astype(jnp.float32))
    for k in range(tiles):
        owner = lax.rem(first[0] + tiles * position + k, owners)
        rows = rows_in[k]
        near = [jnp.sum(grad[2 * k + w], axis=0, keepdims=True) for w in range(2)]
        for group in range(groups):
            to = group * owners + owner
            out[to, :, 2 * LANES : 8 * LANES] = rows[:, 2 * LANES :]
            for w in range(2):
                part = slice(w * LANES, (w + 1) * LANES)
                out[to, :, part] = rows[:, part] + near[w]
            out[to, :, 8 * LANES : 9 * LANES] = start


def join_kernel(received, migrated, total, *, owners, groups):
    position = lax.axis_index("box")
    total[...] = jnp.zeros_like(total)
    for group in range(groups):
        start = received[group * owners, 0, 8 * LANES].astype(jnp.int32)
        base = lax.div(start - position + owners - 1, owners)
        for p in range(owners):
            total[base + p] = total[base + p] + received[group * owners + p, :, 0 : 8 * LANES]
    for r in range(migrated.shape[0]):
        grad = total[r, :, 0 : 4 * LANES]
        illum = total[r, :, 4 * LANES : 8 * LANES]
        image = grad / jnp.sqrt(illum + damping)
        for h in range(2):
            for w in range(2):
                i = 2 * h + w
                migrated[r, 0, w : w + 1, h * LANES : (h + 1) * LANES] = image[
                    :, i * LANES : (i + 1) * LANES
                ]


def on_device(
    u_prev,
    u_now,
    born_prev,
    born_now,
    adj_after,
    adj_last,
    velocity,
    wavelet,
    sources,
    receivers,
    observed,
    first_tile,
    reflectivity,
):
    owners = lax.axis_size("box")
    groups = lax.axis_size("shot")
    columns, depth = velocity.shape[1], velocity.shape[2]
    rounds = reflectivity.shape[0]
    smem, vmem = pl.BlockSpec(memory_space=SMEM), pl.BlockSpec(memory_space=VMEM)
    anywhere = pl.BlockSpec(memory_space=pl.ANY)
    f32 = jnp.float32
    params = pltpu.CompilerParams(vmem_limit_bytes=32 * 1024 * 1024)
    params_hbm = pltpu.CompilerParams(vmem_limit_bytes=60 * 1024 * 1024)
    fields = (u_now, u_prev, born_now, born_prev, adj_last, adj_after)

    pack = jax.ShapeDtypeStruct((PACK_TILES, 8, LANES), f32)
    send_a, send_b, image_out = pl.pallas_call(
        pack_kernel,
        out_shape=(pack, pack, jax.ShapeDtypeStruct((owners, 4, LANES), f32)),
        in_specs=[anywhere] * 11,
        out_specs=(vmem,) * 3,
        scratch_shapes=[
            SMEM(first_tile.shape, jnp.int32),
            SMEM(receivers.shape, jnp.int32),
            VMEM(reflectivity.shape, f32),
            VMEM((2, 4, 8, 8, depth), f32),
            VMEM((2, 2, 8, 8, LANES), f32),
            VMEM((2, 8, depth), f32),
            VMEM(observed.shape, f32),
            pltpu.SemaphoreType.DMA((18,)),
        ],
        compiler_params=params_hbm,
        name="pack",
    )(first_tile, receivers, *fields, velocity, observed, reflectivity)

    ends = (0, owners - 1)
    swap_a = [(i, i ^ 1) for i in range(owners)]
    swap_b = [
        (g * owners + i, (g ^ 1) * owners + i if i in ends else g * owners + (i + 1 if i % 2 else i - 1))
        for g in range(groups)
        for i in range(owners)
    ]
    got_a = lax.ppermute(send_a, "box", swap_a)
    got_b = lax.ppermute(send_b, ("shot", "box"), swap_b)
    image_in = lax.all_to_all(image_out, "box", split_axis=0, concat_axis=0, tiled=True)

    ext = columns + 2 * MARGIN
    shape = jax.ShapeDtypeStruct
    acc, b0, b1, near_speed, meta, rows = pl.pallas_call(
        homogeneous_kernel,
        out_shape=(
            shape((STEPS, ext, 8, LANES), f32),
            shape((ext, 8, LANES), f32),
            shape((ext, 8, LANES), f32),
            shape((ext, 8, LANES), f32),
            shape((2, 8, LANES), f32),
            shape((columns // 2, 1, 8 * LANES), f32),
        ),
        in_specs=[smem] + [vmem] * 10,
        out_specs=(vmem,) * 6,
        scratch_shapes=[VMEM((ext, 8, depth), f32)] * 5 + [VMEM((STEPS, columns, 8, LANES), f32)],
        compiler_params=params,
        name="homogeneous",
    )(sources, *fields, velocity, wavelet, got_a, got_b)
    out = pl.pallas_call(
        functools.partial(scattered_kernel, owners=owners, groups=groups, depth=depth),
        out_shape=shape((groups * owners, 1, 9 * LANES), f32),
        in_specs=[smem] * 2 + [vmem] * 8,
        out_specs=vmem,
        scratch_shapes=[VMEM((ext, 8, LANES), f32)] * 5,
        compiler_params=params,
        name="scattered",
    )(
        first_tile,
        receivers,
        acc,
        b0,
        b1,
        near_speed,
        meta,
        rows,
        observed,
        image_in,
    )

    received = lax.all_to_all(out, ("shot", "box"), split_axis=0, concat_axis=0, tiled=True)
    return pl.pallas_call(
        functools.partial(join_kernel, owners=owners, groups=groups),
        out_shape=jax.ShapeDtypeStruct(reflectivity.shape, f32),
        in_specs=[vmem],
        out_specs=vmem,
        scratch_shapes=[VMEM((rounds, 1, 8 * LANES), f32)],
        compiler_params=params,
        name="join",
    )(received)


def solution(mesh):
    return jax.shard_map(
        on_device,
        mesh=mesh,
        in_specs=(
            P("shot", None, "box", None),
            P("shot", None, "box", None),
            P("shot", None, "box", None),
            P("shot", None, "box", None),
            P("shot", None, "box", None),
            P("shot", None, "box", None),
            P("shot", "box", None),
            P("shot", None, None),
            P("shot", None),
            P("shot", "box"),
            P("shot", None, None, "box"),
            P("shot"),
            P(None, "box", None, None),
        ),
        out_specs=P(None, "box", None, None),
        check_vma=False,
    )
```

```python
import functools

import jax
import jax.numpy as jnp
from jax import lax
from jax.experimental import pallas as pl
from jax.experimental.pallas import tpu as pltpu
from jax.sharding import PartitionSpec as P

damping = 1.0
LANES = 128
MARGIN = 8
STEPS = 4
HALO = (
    ("un", 0, 7),
    ("up", 0, 6),
    ("bn", 0, 7),
    ("bp", 0, 6),
    ("un", 1, 4),
    ("up", 1, 3),
    ("qn", 0, 4),
    ("qn", 1, 4),
    ("qp", 0, 3),
    ("qp", 1, 3),
)
HALO_TILES = sum(count for _, _, count in HALO)
SPEED_TILE = HALO_TILES
META_TILE = HALO_TILES + 2
PACK_TILES = HALO_TILES + 3
VMEM = pltpu.VMEM
SMEM = pltpu.SMEM


def lane_iota():
    return lax.broadcasted_iota(jnp.int32, (8, LANES), 1)


def choose_kernel(first, own, other, info_in, info, *picks, columns):
    info[...] = info_in[...]
    info[0] = jnp.full((8, LANES), first[0])
    position = lax.axis_index("box")
    owners = 2 * len(picks)
    rounds = own.shape[0]
    for i, pick in enumerate(picks):
        target = position ^ (2 * i)
        low_tile = first[0] + (columns // 2) * target - 3
        for core, tiles in enumerate((own, other)):
            owner = position ^ core
            r0 = lax.div(low_tile - owner + 2 * owners - 1, owners) - 1
            for slot in range(2):
                r = jnp.clip(r0 + slot, 0, rounds - 1)
                pick[core, 2 * slot : 2 * slot + 2, :] = tiles[r, 0, :, 0:LANES]


def pack_kernel(
    sources_any,
    rec_any,
    un,
    up,
    bn,
    bp,
    qn,
    qp,
    speed_any,
    obs_any,
    pack_a,
    pack_b,
    info,
    sources,
    rec,
    wide,
    near,
    speed,
    obs,
    sems,
):
    columns, depth = un.shape[2], un.shape[3]
    position = lax.axis_index("box")
    even = lax.rem(position, 2) == 0
    lane = lane_iota()
    row = lax.broadcasted_iota(jnp.int32, (8, LANES), 0)
    edges = (pl.ds(0, 8), pl.ds(columns - 8, 8))
    wides = {"un": 0, "up": 1, "qn": 2, "qp": 3}
    nears = {"bn": 0, "bp": 1}
    fields = {"un": un, "up": up, "bn": bn, "bp": bp, "qn": qn, "qp": qp}

    moves = [[(sources_any, sources), (rec_any, rec)]]
    for name, ref in fields.items():
        group = []
        for side in range(2):
            if name in wides:
                group.append((ref.at[0, :, edges[side], :], wide.at[side, wides[name]]))
            else:
                source = ref.at[0, :, edges[side], pl.ds(0, LANES)]
                group.append((source, near.at[side, nears[name]]))
        moves.append(group)
    moves.append([(speed_any.at[0, edges[side], :], speed.at[side]) for side in range(2)])
    moves[-1].append((obs_any, obs))
    copies, i = [], 0
    for group in moves:
        copies.append([])
        for move in group:
            copies[-1].append(pltpu.make_async_copy(*move, sems.at[i]))
            copies[-1][-1].start()
            i += 1

    def arrive(group):
        for copy in copies[group]:
            copy.wait()

    arrive(0)
    own_cell = position * columns * depth
    info[0] = jnp.zeros((8, LANES), jnp.int32)
    cell = jnp.zeros((8, LANES), jnp.int32)
    for s in range(8):
        cell = jnp.where(row == s, sources[0, s] - own_cell, cell)
    info[1] = cell
    count = rec.shape[1]
    for block in range(0, count, 8):
        cell = jnp.zeros((8, LANES), jnp.int32)
        for r in range(min(8, count - block)):
            cell = jnp.where(row == r, rec[0, block + r] - own_cell, cell)
        info[2 + block // 8] = cell

    def put(tile, left, right):
        pack_a[tile] = jnp.where(even, right, left)
        pack_b[tile] = jnp.where(even, left, right)

    arrived, tile = set(), 0
    for name, half, width in HALO:
        if name not in arrived:
            arrive(1 + list(fields).index(name))
            arrived.add(name)
        part = slice(half * LANES, (half + 1) * LANES)
        if name in nears:
            low, high = (near[side, nears[name]] for side in range(2))
        else:
            low, high = (wide[side, wides[name], :, :, part] for side in range(2))
        low, high = jnp.swapaxes(low, 0, 1), jnp.swapaxes(high, 0, 1)
        for j in range(1, width + 1):
            put(tile, low[j - 1], high[8 - j])
            tile += 1
    arrive(1 + len(fields))
    for half in range(2):
        part = slice(half * LANES, (half + 1) * LANES)
        put(SPEED_TILE + half, speed[0, :, part], speed[1, :, part])

    def meta(right):
        out = jnp.zeros((8, LANES), jnp.float32)
        for k in range(2):
            r = count - 1 - k if right else k
            for t in range(STEPS):
                value = jnp.broadcast_to(obs[0, :, t, r : r + 1], (8, LANES))
                out = jnp.where(lane == 2 * t + k, value, out)
            column = lax.div(rec[0, r], depth) - position * columns
            distance = columns - column if right else column + 1
            code = distance * depth + lax.rem(rec[0, r], depth)
            out = jnp.where(lane == 2 * STEPS + k, code.astype(jnp.float32), out)
        return out

    put(META_TILE, meta(False), meta(True))


def depthwise(xs, first_lane, last_lane):
    rolled_up = [pltpu.roll(x, 1, 1) for x in xs]
    rolled_down = [pltpu.roll(x, LANES - 1, 1) for x in xs]
    if len(xs) == 1:
        return [
            jnp.where(first_lane, 0.0, rolled_up[0]) + jnp.where(last_lane, 0.0, rolled_down[0])
        ]
    return [
        jnp.where(first_lane, 0.0, rolled_up[0])
        + jnp.where(last_lane, rolled_down[1], rolled_down[0]),
        jnp.where(first_lane, rolled_up[0], rolled_up[1])
        + jnp.where(last_lane, 0.0, rolled_down[1]),
    ]


def lap(ref, e, count, edges):
    parts = [slice(h * LANES, (h + 1) * LANES) for h in range(count)]
    mid = [ref[e, :, part] for part in parts]
    along = depthwise(mid, *edges)
    return mid, [
        ref[e - 1, :, parts[h]] + ref[e + 1, :, parts[h]] + along[h] - 4.0 * mid[h]
        for h in range(count)
    ]


def homogeneous_kernel(
    info,
    un,
    up,
    bn,
    bp,
    qn,
    qp,
    speed,
    obs,
    wavelet,
    pack_a,
    pack_b,
    acc,
    near_speed,
    hit_out,
    ahead,
    out,
    u0,
    u1,
    b0,
    b1,
    q0,
    q1,
    vel,
    late,
    *,
    owners,
    groups,
):
    columns, depth = speed.shape[1], speed.shape[2]
    tiles = columns // 2
    position = lax.axis_index("box")
    even = lax.rem(position, 2) == 0
    has_left = position > 0
    has_right = position < owners - 1
    lane = lane_iota()
    edges = lane == 0, lane == LANES - 1
    zero = jnp.zeros((8, LANES), jnp.float32)
    halves = (slice(0, LANES), slice(LANES, 2 * LANES))
    scratch = {"un": u0, "up": u1, "bn": b0, "bp": b1, "qn": q0, "qp": q1}
    first = info[0, 0, 0]

    for name, ref in (("un", un), ("up", up), ("qn", qn), ("qp", qp)):
        for c in range(0, columns, 8):
            scratch[name][MARGIN + c : MARGIN + c + 8] = jnp.swapaxes(ref[0, :, c : c + 8, :], 0, 1)
    for name, ref in (("bn", bn), ("bp", bp)):
        for c in range(0, columns, 8):
            scratch[name][MARGIN + c : MARGIN + c + 8] = jnp.swapaxes(
                ref[0, :, c : c + 8, 0:LANES], 0, 1
            )
    for c in range(columns):
        vel[MARGIN + c] = jnp.broadcast_to(speed[0, c : c + 1, :], (8, depth))

    def got(tile):
        a, b = pack_a[tile], pack_b[tile]
        left, right = jnp.where(even, b, a), jnp.where(even, a, b)
        return jnp.where(has_left, left, 0.0), jnp.where(has_right, right, 0.0)

    tile = 0
    for name, half, count in HALO:
        for j in range(1, count + 1):
            left, right = got(tile)
            scratch[name][MARGIN - j, :, halves[half]] = left
            scratch[name][MARGIN + columns - 1 + j, :, halves[half]] = right
            tile += 1
    for half, count in ((0, 6), (1, 3)):
        left, right = got(SPEED_TILE + half)
        for j in range(1, count + 1):
            vel[MARGIN - j, :, halves[half]] = jnp.broadcast_to(left[8 - j : 9 - j], (8, LANES))
            vel[MARGIN + columns - 1 + j, :, halves[half]] = jnp.broadcast_to(
                right[j - 1 : j], (8, LANES)
            )
    meta = got(META_TILE)
    for c in range(-6, columns + 6):
        near_speed[MARGIN + c] = vel[MARGIN + c, :, halves[0]]

    cell = info[1] - lane
    pulses = [jnp.broadcast_to(wavelet[0, :, t : t + 1], (8, LANES)) for t in range(STEPS)]
    new_u, old_u = u0, u1
    illum = [[zero, zero] for _ in range(columns)]
    for t in range(STEPS):
        wide, narrow = 6 - t, 3 - t
        for c in range(-wide, columns + wide):
            e = MARGIN + c
            count = 2 if -narrow <= c < columns + narrow else 1
            mid, laps = lap(new_u, e, count, edges)
            for h in range(count):
                hit = cell == c * depth + h * LANES
                a = vel[e, :, halves[h]] * laps[h] + jnp.where(hit, pulses[t], 0.0)
                if h == 0:
                    acc[t, e] = a
                elif 0 <= c < columns:
                    late[t, c] = a
                old_u[e, :, halves[h]] = 2.0 * mid[h] - old_u[e, :, halves[h]] + a
                if 0 <= c < columns:
                    illum[c][h] = illum[c][h] + a * a
        new_u, old_u = old_u, new_u

    reach = STEPS - 1
    recorded = {}
    for c in range(-reach, columns + reach):
        if 0 <= c < columns:
            r = c // 2
            here = jnp.broadcast_to(info[2 + r // 8, r % 8 : r % 8 + 1, :], (8, LANES))
            hit = lane == here - c * depth
            columns_of = [obs[0, :, t, r : r + 1] for t in range(STEPS)]
        else:
            j = -c if c < 0 else c - columns + 1
            side, k = meta[0] if c < 0 else meta[1], (j - 1) // 2
            code = jnp.broadcast_to(side[:, 2 * STEPS + k : 2 * STEPS + k + 1], (8, LANES))
            hit = code == (lane + j * depth).astype(jnp.float32)
            columns_of = [side[:, 2 * t + k : 2 * t + k + 1] for t in range(STEPS)]
        hit_out[reach + c] = jnp.where(hit, 1.0, 0.0)
        recorded[c] = columns_of
    new_b, old_b = b0, b1
    for t in range(STEPS):
        wide = 2 * reach - t
        for c in range(-wide, columns + wide):
            e = MARGIN + c
            (mid,), (laps,) = lap(new_b, e, 1, edges)
            b = 2.0 * mid - old_b[e] + vel[e, :, halves[0]] * laps
            old_b[e] = b
            if -t <= c < columns + t:
                value = jnp.broadcast_to(recorded[c][t], (8, LANES))
                ahead[t, reach + c] = hit_out[reach + c] * (b - value)
        new_b, old_b = old_b, new_b

    grad = [[zero, zero] for _ in range(columns)]
    new_q, old_q = q0, q1
    for t in reversed(range(STEPS)):
        for c in range(-t, columns + t):
            e = MARGIN + c
            mid, laps = lap(new_q, e, 2, edges)
            for h in range(2):
                q = 2.0 * mid[h] - old_q[e, :, halves[h]] + vel[e, :, halves[h]] * laps[h]
                old_q[e, :, halves[h]] = q
                if 0 <= c < columns:
                    a = late[t, c] if h else acc[t, e]
                    grad[c][h] = grad[c][h] + q * a
        new_q, old_q = old_q, new_q

    start = jnp.full((1, LANES), first.astype(jnp.float32))
    for k in range(tiles):
        owner = lax.rem(first + tiles * position + k, owners)
        i = 0
        for sums in (grad, illum):
            for h in range(2):
                for w in range(2):
                    total = jnp.sum(sums[2 * k + w][h], axis=0, keepdims=True)
                    for group in range(groups):
                        out[group * owners + owner, :, i * LANES : (i + 1) * LANES] = total
                    i += 1
        for group in range(groups):
            out[group * owners + owner, :, 8 * LANES : 9 * LANES] = start


def scattered_kernel(
    info,
    acc,
    speed,
    hit,
    ahead,
    *refs,
    owners,
    groups,
):
    images, (_, out, b0, b1, q0, q1, img) = refs[: owners // 2], refs[owners // 2 :]
    reach = STEPS - 1
    columns = hit.shape[0] - 2 * reach
    tiles = columns // 2
    position = lax.axis_index("box")
    lane = lane_iota()
    edges = lane == 0, lane == LANES - 1
    zero = jnp.zeros((8, LANES), jnp.float32)
    first = info[0, 0, 0]

    low_tile = first + tiles * position - 3 + owners
    for m in range(tiles + 6):
        apart = lax.rem(low_tile + m, owners) ^ position
        chips, core = lax.div(apart, 2), lax.rem(apart, 2)
        part = slice(2 * (m // owners), 2 * (m // owners) + 2)
        pair = images[0][core, part, :]
        for i in range(1, owners // 2):
            pair = jnp.where(chips == i, images[i][core, part, :], pair)
        for w in range(2):
            img[MARGIN - 6 + 2 * m + w] = jnp.broadcast_to(pair[w : w + 1], (8, LANES))

    misfits = []
    new_b, old_b = b0, b1
    for t in range(STEPS):
        wide = 2 * reach - t
        for c in range(-wide, columns + wide):
            e = MARGIN + c
            b = img[e] * acc[t, e]
            if t > 0:
                (mid,), (laps,) = lap(new_b, e, 1, edges)
                b = b + 2.0 * mid + speed[e] * laps
            if t > 1:
                b = b - old_b[e]
            old_b[e] = b
        new_b, old_b = old_b, new_b
        misfits.append(
            {
                c: hit[reach + c] * new_b[MARGIN + c] + ahead[t, reach + c]
                for c in range(-t, columns + t)
            }
        )

    grad = [zero] * columns
    new_q, old_q = q0, q1
    for t in reversed(range(STEPS)):
        for c in range(-t, columns + t):
            e = MARGIN + c
            q = misfits[t][c]
            if t < STEPS - 1:
                (mid,), (laps,) = lap(new_q, e, 1, edges)
                q = q + 2.0 * mid + speed[e] * laps
            if t < STEPS - 2:
                q = q - old_q[e]
            old_q[e] = q
            if 0 <= c < columns:
                grad[c] = grad[c] + q * acc[t, e]
        new_q, old_q = old_q, new_q

    for k in range(tiles):
        owner = lax.rem(first + tiles * position + k, owners)
        for w in range(2):
            part = slice(w * LANES, (w + 1) * LANES)
            total = out[owner, :, part] + jnp.sum(grad[2 * k + w], axis=0, keepdims=True)
            for group in range(groups):
                out[group * owners + owner, :, part] = total


def join_kernel(received, migrated, total, *, owners, groups):
    position = lax.axis_index("box")
    total[...] = jnp.zeros_like(total)
    for group in range(groups):
        start = received[group * owners, 0, 8 * LANES].astype(jnp.int32)
        base = lax.div(start - position + owners - 1, owners)
        for p in range(owners):
            total[base + p] = total[base + p] + received[group * owners + p, :, 0 : 8 * LANES]
    for r in range(migrated.shape[0]):
        grad = total[r, :, 0 : 4 * LANES]
        illum = total[r, :, 4 * LANES : 8 * LANES]
        image = grad / jnp.sqrt(illum + damping)
        for h in range(2):
            for w in range(2):
                i = 2 * h + w
                migrated[r, 0, w : w + 1, h * LANES : (h + 1) * LANES] = image[
                    :, i * LANES : (i + 1) * LANES
                ]


def on_device(
    u_prev,
    u_now,
    born_prev,
    born_now,
    adj_after,
    adj_last,
    velocity,
    wavelet,
    sources,
    receivers,
    observed,
    first_tile,
    reflectivity,
):
    owners = lax.axis_size("box")
    groups = lax.axis_size("shot")
    columns, depth = velocity.shape[1], velocity.shape[2]
    rounds = reflectivity.shape[0]
    vmem = pl.BlockSpec(memory_space=VMEM)
    anywhere = pl.BlockSpec(memory_space=pl.ANY)
    f32 = jnp.float32
    params = pltpu.CompilerParams(vmem_limit_bytes=24 * 1024 * 1024)
    params_hbm = pltpu.CompilerParams(vmem_limit_bytes=24 * 1024 * 1024)
    fields = (u_now, u_prev, born_now, born_prev, adj_last, adj_after)

    shape = jax.ShapeDtypeStruct
    pack = VMEM((PACK_TILES, 8, LANES), f32)
    blocks = 2 + pl.cdiv(receivers.shape[1], 8)
    pack_from = (sources, receivers, *fields, velocity, observed)
    send_a, send_b, info = pl.pallas_call(
        pack_kernel,
        out_shape=(
            pack,
            pack,
            VMEM((blocks, 8, LANES), jnp.int32),
        ),
        in_specs=[anywhere] * 10,
        out_specs=(vmem,) * 3,
        scratch_shapes=[
            SMEM(sources.shape, jnp.int32),
            SMEM(receivers.shape, jnp.int32),
            VMEM((2, 4, 8, 8, depth), f32),
            VMEM((2, 2, 8, 8, LANES), f32),
            VMEM((2, 8, depth), f32),
            VMEM(observed.shape, f32),
            pltpu.SemaphoreType.DMA((17,)),
        ],
        compiler_params=params_hbm,
        name="pack",
    )(*(pltpu.with_memory_space_constraint(x, pltpu.HBM) for x in pack_from))
    ends = (0, owners - 1)
    swap_a = [(i, i ^ 1) for i in range(owners)]
    swap_b = [
        (g * owners + i, (g ^ 1) * owners + i if i in ends else g * owners + (i + 1 if i % 2 else i - 1))
        for g in range(groups)
        for i in range(owners)
    ]
    got_a = lax.ppermute(send_a, "box", swap_a)
    got_b = lax.ppermute(send_b, ("shot", "box"), swap_b)
    other_image = lax.ppermute(reflectivity, "box", swap_a)
    info, *picks = pl.pallas_call(
        functools.partial(choose_kernel, columns=columns),
        out_shape=(VMEM((blocks, 8, LANES), jnp.int32),)
        + (VMEM((2, 4, LANES), f32),) * (owners // 2),
        in_specs=[pl.BlockSpec(memory_space=SMEM)] + [vmem] * 3,
        out_specs=(vmem,) * (1 + owners // 2),
        compiler_params=params,
        name="choose",
    )(first_tile, reflectivity, other_image, info)
    images = [picks[0]] + [
        lax.ppermute(picks[i], "box", [(j, j ^ (2 * i)) for j in range(owners)])
        for i in range(1, owners // 2)
    ]

    ext = columns + 2 * MARGIN
    near = columns + 2 * (STEPS - 1)
    payload = shape((groups * owners, 1, 9 * LANES), f32)
    acc, near_speed, hit, ahead, part = pl.pallas_call(
        functools.partial(homogeneous_kernel, owners=owners, groups=groups),
        out_shape=(
            shape((STEPS, ext, 8, LANES), f32),
            shape((ext, 8, LANES), f32),
            shape((near, 8, LANES), f32),
            shape((STEPS, near, 8, LANES), f32),
            payload,
        ),
        in_specs=[vmem] * 12,
        out_specs=(vmem,) * 5,
        scratch_shapes=[VMEM((ext, 8, depth), f32)] * 2
        + [VMEM((ext, 8, LANES), f32)] * 2
        + [VMEM((ext, 8, depth), f32)] * 3
        + [VMEM((STEPS, columns, 8, LANES), f32)],
        compiler_params=params,
        name="homogeneous",
    )(info, *fields, velocity, observed, wavelet, got_a, got_b)
    out = pl.pallas_call(
        functools.partial(scattered_kernel, owners=owners, groups=groups),
        out_shape=payload,
        in_specs=[vmem] * (6 + len(images)),
        out_specs=vmem,
        scratch_shapes=[VMEM((ext, 8, LANES), f32)] * 5,
        input_output_aliases={5 + len(images): 0},
        compiler_params=params,
        name="scattered",
    )(info, acc, near_speed, hit, ahead, *images, part)

    received = lax.all_to_all(out, ("shot", "box"), split_axis=0, concat_axis=0, tiled=True)
    return pl.pallas_call(
        functools.partial(join_kernel, owners=owners, groups=groups),
        out_shape=jax.ShapeDtypeStruct(reflectivity.shape, f32),
        in_specs=[vmem],
        out_specs=vmem,
        scratch_shapes=[VMEM((rounds, 1, 8 * LANES), f32)],
        compiler_params=params,
        name="join",
    )(received)


def solution(mesh):
    return jax.shard_map(
        on_device,
        mesh=mesh,
        in_specs=(
            P("shot", None, "box", None),
            P("shot", None, "box", None),
            P("shot", None, "box", None),
            P("shot", None, "box", None),
            P("shot", None, "box", None),
            P("shot", None, "box", None),
            P("shot", "box", None),
            P("shot", None, None),
            P("shot", None),
            P("shot", "box"),
            P("shot", None, None, "box"),
            P("shot"),
            P(None, "box", None, None),
        ),
        out_specs=P(None, "box", None, None),
        check_vma=False,
    )
```

```python
import functools

import jax
import jax.numpy as jnp
from jax import lax
from jax.experimental import pallas as pl
from jax.experimental.pallas import tpu as pltpu
from jax.sharding import PartitionSpec as P

damping = 1.0
LANES = 128
MARGIN = 8
STEPS = 4
HALO = (
    ("un", 0, 7),
    ("up", 0, 6),
    ("bn", 0, 7),
    ("bp", 0, 6),
    ("un", 1, 4),
    ("up", 1, 3),
    ("qn", 0, 4),
    ("qn", 1, 4),
    ("qp", 0, 3),
    ("qp", 1, 3),
)
HALO_TILES = sum(count for _, _, count in HALO)
SPEED_TILE = HALO_TILES
META_TILE = HALO_TILES + 2
PACK_TILES = HALO_TILES + 3
VMEM = pltpu.VMEM
SMEM = pltpu.SMEM


def partner_bits(i):
    return 2 * i + 1 if i else 0


def lane_iota():
    return lax.broadcasted_iota(jnp.int32, (8, LANES), 1)


def choose_kernel(first, own, pack_a, info_in, info, *picks, columns):
    info[...] = info_in[...]
    info[0] = jnp.full((8, LANES), first[0])
    start = first[0]
    position = lax.axis_index("box")
    owners = 2 * len(picks)
    rounds = own.shape[0]
    for i, pick in enumerate(picks):
        target = position ^ partner_bits(i)
        low_tile = start + (columns // 2) * target - 3
        for core in range(2):
            owner = position ^ core
            r0 = lax.div(low_tile - owner + 2 * owners - 1, owners) - 1
            for slot in range(2):
                r = jnp.clip(r0 + slot, 0, rounds - 1)
                if core == 0:
                    tile = own[r, 0, :, 0:LANES]
                else:
                    row = pl.multiple_of(2 * lax.rem(r, 4), 2)
                    tile = pack_a[PACK_TILES + lax.div(r, 4), pl.ds(row, 2), :]
                pick[core, 2 * slot : 2 * slot + 2, :] = tile


def pack_kernel(
    sources_any,
    rec_any,
    un,
    up,
    bn,
    bp,
    qn,
    qp,
    speed_any,
    obs_any,
    refl_any,
    pack_a,
    pack_b,
    info,
    sources,
    rec,
    refl,
    wide,
    near,
    speed,
    obs,
    sems,
):
    columns, depth = un.shape[2], un.shape[3]
    position = lax.axis_index("box")
    even = lax.rem(position, 2) == 0
    lane = lane_iota()
    row = lax.broadcasted_iota(jnp.int32, (8, LANES), 0)
    edges = (pl.ds(0, 8), pl.ds(columns - 8, 8))
    wides = {"un": 0, "up": 1, "qn": 2, "qp": 3}
    nears = {"bn": 0, "bp": 1}
    fields = {"un": un, "up": up, "bn": bn, "bp": bp, "qn": qn, "qp": qp}

    moves = [[(sources_any, sources), (rec_any, rec)]]
    for name, ref in fields.items():
        group = []
        for side in range(2):
            if name in wides:
                group.append((ref.at[0, :, edges[side], :], wide.at[side, wides[name]]))
            else:
                source = ref.at[0, :, edges[side], pl.ds(0, LANES)]
                group.append((source, near.at[side, nears[name]]))
        moves.append(group)
    moves.append([(speed_any.at[0, edges[side], :], speed.at[side]) for side in range(2)])
    moves[-1].append((obs_any, obs))
    moves.append([(refl_any, refl)])
    copies, i = [], 0
    for group in moves:
        copies.append([])
        for move in group:
            copies[-1].append(pltpu.make_async_copy(*move, sems.at[i]))
            copies[-1][-1].start()
            i += 1

    def arrive(group):
        for copy in copies[group]:
            copy.wait()

    for group in range(len(copies)):
        arrive(group)
    own_cell = position * columns * depth
    info[0] = jnp.zeros((8, LANES), jnp.int32)
    cell = jnp.zeros((8, LANES), jnp.int32)
    for s in range(8):
        cell = jnp.where(row == s, sources[0, s] - own_cell, cell)
    info[1] = cell
    count = rec.shape[1]
    edge_receivers = (0, 1, count - 1, count - 2)
    for block in range(0, count, 8):
        cell = jnp.zeros((8, LANES), jnp.int32)
        for r in range(min(8, count - block)):
            cell = jnp.where(row == r, rec[0, block + r] - own_cell, cell)
        info[2 + block // 8] = cell

    def send(low_to, high_to):
        def put(tile, low, high):
            if low_to is not None:
                low_to[tile] = low
            if high_to is not None:
                high_to[tile] = high

        tile = 0
        for name, half, width in HALO:
            part = slice(half * LANES, (half + 1) * LANES)
            if name in nears:
                low, high = (near[side, nears[name]] for side in range(2))
            else:
                low, high = (wide[side, wides[name], :, :, part] for side in range(2))
            low, high = jnp.swapaxes(low, 0, 1), jnp.swapaxes(high, 0, 1)
            for j in range(1, width + 1):
                put(tile, low[j - 1], high[8 - j])
                tile += 1
        for half in range(2):
            part = slice(half * LANES, (half + 1) * LANES)
            put(SPEED_TILE + half, speed[0, :, part], speed[1, :, part])
        put(META_TILE, meta[0], meta[1])

    recorded = []
    for t in range(STEPS):
        at = obs[0, :, t, :]
        recorded.append([jnp.broadcast_to(at[:, r : r + 1], (8, LANES)) for r in edge_receivers])
    meta = []
    for side in range(2):
        out = jnp.zeros((8, LANES), jnp.float32)
        for k in range(2):
            r = edge_receivers[2 * side + k]
            for t in range(STEPS):
                out = jnp.where(lane == 2 * t + k, recorded[t][2 * side + k], out)
            column = lax.div(rec[0, r], depth) - position * columns
            distance = columns - column if side else column + 1
            code = distance * depth + lax.rem(rec[0, r], depth)
            out = jnp.where(lane == 2 * STEPS + k, code.astype(jnp.float32), out)
        meta.append(out)

    is_end = jnp.logical_or(position == 0, position == lax.axis_size("box") - 1)

    @pl.when(jnp.logical_and(even, jnp.logical_not(is_end)))
    def _():
        send(pack_b, pack_a)

    @pl.when(jnp.logical_and(jnp.logical_not(even), jnp.logical_not(is_end)))
    def _():
        send(pack_a, pack_b)

    @pl.when(is_end)
    def _():
        pack_b[...] = jnp.zeros_like(pack_b)

    @pl.when(jnp.logical_and(even, is_end))
    def _():
        send(None, pack_a)

    @pl.when(jnp.logical_and(jnp.logical_not(even), is_end))
    def _():
        send(pack_a, None)

    for r in range(refl.shape[0]):
        row = 2 * (r % 4)
        pack_a[PACK_TILES + r // 4, row : row + 2, :] = refl[r, 0, :, 0:LANES]


def depthwise(xs, first_lane, last_lane):
    rolled_up = [pltpu.roll(x, 1, 1) for x in xs]
    rolled_down = [pltpu.roll(x, LANES - 1, 1) for x in xs]
    if len(xs) == 1:
        return [
            jnp.where(first_lane, 0.0, rolled_up[0]) + jnp.where(last_lane, 0.0, rolled_down[0])
        ]
    return [
        jnp.where(first_lane, 0.0, rolled_up[0])
        + jnp.where(last_lane, rolled_down[1], rolled_down[0]),
        jnp.where(first_lane, rolled_up[0], rolled_up[1])
        + jnp.where(last_lane, 0.0, rolled_down[1]),
    ]


def lap(ref, e, count, edges):
    parts = [slice(h * LANES, (h + 1) * LANES) for h in range(count)]
    mid = [ref[e, :, part] for part in parts]
    along = depthwise(mid, *edges)
    return mid, [
        ref[e - 1, :, parts[h]] + ref[e + 1, :, parts[h]] + along[h] - 4.0 * mid[h]
        for h in range(count)
    ]


def homogeneous_kernel(
    info,
    un,
    up,
    bn,
    bp,
    qn,
    qp,
    speed,
    obs,
    wavelet,
    pack_a,
    pack_b,
    acc,
    near_speed,
    hit_out,
    ahead,
    out,
    u0,
    u1,
    b0,
    b1,
    q0,
    q1,
    q2,
    q3,
    q4,
    vel,
    late,
    metas,
    *,
    owners,
    groups,
):
    columns, depth = speed.shape[1], speed.shape[2]
    tiles = columns // 2
    position = lax.axis_index("box")
    even = lax.rem(position, 2) == 0
    lane = lane_iota()
    edges = lane == 0, lane == LANES - 1
    halves = (slice(0, LANES), slice(LANES, 2 * LANES))
    scratch = {"un": u0, "up": u1, "bn": b0, "bp": b1, "qn": q0, "qp": q1}
    first = info[0, 0, 0]

    for name, ref in (("un", un), ("up", up), ("qn", qn), ("qp", qp)):
        for c in range(0, columns, 8):
            scratch[name][MARGIN + c : MARGIN + c + 8] = jnp.swapaxes(ref[0, :, c : c + 8, :], 0, 1)
    for name, ref in (("bn", bn), ("bp", bp)):
        for c in range(0, columns, 8):
            scratch[name][MARGIN + c : MARGIN + c + 8] = jnp.swapaxes(
                ref[0, :, c : c + 8, 0:LANES], 0, 1
            )
    for c in range(columns):
        vel[MARGIN + c] = jnp.broadcast_to(speed[0, c : c + 1, :], (8, depth))
        near_speed[MARGIN + c] = vel[MARGIN + c, :, halves[0]]

    def receive(left, right):
        tile = 0
        for name, half, count in HALO:
            for j in range(1, count + 1):
                scratch[name][MARGIN - j, :, halves[half]] = left[tile]
                scratch[name][MARGIN + columns - 1 + j, :, halves[half]] = right[tile]
                tile += 1
        for half, count in ((0, 6), (1, 3)):
            for j in range(1, count + 1):
                for e, v in (
                    (MARGIN - j, left[SPEED_TILE + half, 8 - j : 9 - j, :]),
                    (MARGIN + columns - 1 + j, right[SPEED_TILE + half, j - 1 : j, :]),
                ):
                    v = jnp.broadcast_to(v, (8, LANES))
                    vel[e, :, halves[half]] = v
                    if half == 0:
                        near_speed[e] = v
        metas[0] = left[META_TILE]
        metas[1] = right[META_TILE]

    @pl.when(even)
    def _():
        receive(pack_b, pack_a)

    @pl.when(jnp.logical_not(even))
    def _():
        receive(pack_a, pack_b)

    meta = metas[0], metas[1]

    cell = info[1] - lane
    pulses = [jnp.broadcast_to(wavelet[0, :, t : t + 1], (8, LANES)) for t in range(STEPS)]
    new_u, old_u = u0, u1
    for t in range(STEPS):
        wide, narrow = 6 - t, 3 - t
        for c in range(-wide, columns + wide):
            e = MARGIN + c
            count = 2 if -narrow <= c < columns + narrow else 1
            mid, laps = lap(new_u, e, count, edges)
            for h in range(count):
                hit = cell == c * depth + h * LANES
                a = vel[e, :, halves[h]] * laps[h] + jnp.where(hit, pulses[t], 0.0)
                if h == 0:
                    acc[t, e] = a
                elif 0 <= c < columns:
                    late[t, c] = a
                if t < STEPS - 1:
                    old_u[e, :, halves[h]] = 2.0 * mid[h] - old_u[e, :, halves[h]] + a
        new_u, old_u = old_u, new_u

    reach = STEPS - 1
    recorded = {}
    own_obs = [obs[0, :, t, :] for t in range(STEPS)]
    for c in range(-reach, columns + reach):
        if 0 <= c < columns:
            r = c // 2
            here = jnp.broadcast_to(info[2 + r // 8, r % 8 : r % 8 + 1, :], (8, LANES))
            hit = lane == here - c * depth
            if c % 2 == 0:
                pair = [jnp.broadcast_to(at[:, r : r + 1], (8, LANES)) for at in own_obs]
            recorded[c] = pair
        else:
            j = -c if c < 0 else c - columns + 1
            side, k = meta[0] if c < 0 else meta[1], (j - 1) // 2
            code = jnp.broadcast_to(side[:, 2 * STEPS + k : 2 * STEPS + k + 1], (8, LANES))
            hit = code == (lane + j * depth).astype(jnp.float32)
            recorded[c] = [
                jnp.broadcast_to(side[:, 2 * t + k : 2 * t + k + 1], (8, LANES))
                for t in range(STEPS)
            ]
        hit_out[reach + c] = jnp.where(hit, 1.0, 0.0)
        for t in range(STEPS):
            if -t <= c < columns + t:
                ahead[t, reach + c] = recorded[c][t]
    new_b, old_b = b0, b1
    for t in range(STEPS):
        wide = 2 * reach - t
        for c in range(-wide, columns + wide):
            e = MARGIN + c
            (mid,), (laps,) = lap(new_b, e, 1, edges)
            b = 2.0 * mid - old_b[e] + vel[e, :, halves[0]] * laps
            if t < STEPS - 1:
                old_b[e] = b
            if -t <= c < columns + t:
                ahead[t, reach + c] = hit_out[reach + c] * (b - ahead[t, reach + c])
        new_b, old_b = old_b, new_b

    newer, older = q0, q1
    for t, q_t in zip(reversed(range(STEPS)), (q2, q3, q4, q1)):
        for c in range(-t, columns + t):
            e = MARGIN + c
            mid, laps = lap(newer, e, 2, edges)
            for h in range(2):
                q_t[e, :, halves[h]] = (
                    2.0 * mid[h] - older[e, :, halves[h]] + vel[e, :, halves[h]] * laps[h]
                )
        newer, older = q_t, newer
    adjoint = (q1, q4, q3, q2)

    start = jnp.full((1, LANES), first.astype(jnp.float32))
    for k in range(tiles):
        owner = lax.rem(first + tiles * position + k, owners)
        grads, illums = [], []
        for h in range(2):
            for w in range(2):
                c = 2 * k + w
                grad = illum = None
                for t in range(STEPS):
                    a = late[t, c] if h else acc[t, MARGIN + c]
                    g = adjoint[t][MARGIN + c, :, halves[h]] * a
                    grad = g if grad is None else grad + g
                    illum = a * a if illum is None else illum + a * a
                grads.append(grad)
                illums.append(illum)
        for i, total in enumerate(grads + illums):
            total = jnp.sum(total, axis=0, keepdims=True)
            for group in range(groups):
                out[group * owners + owner, :, i * LANES : (i + 1) * LANES] = total
        for group in range(groups):
            out[group * owners + owner, :, 8 * LANES : 9 * LANES] = start


def scattered_kernel(
    info,
    acc,
    speed,
    hit,
    ahead,
    *refs,
    owners,
    groups,
):
    images, (_, out, b0, b1, q0, q1, q2, q3, img) = refs[: owners // 2], refs[owners // 2 :]
    reach = STEPS - 1
    columns = hit.shape[0] - 2 * reach
    tiles = columns // 2
    position = lax.axis_index("box")
    lane = lane_iota()
    edges = lane == 0, lane == LANES - 1
    first = info[0, 0, 0]

    low_tile = first + tiles * position - 3 + owners
    for m in range(tiles + 6):
        apart = lax.rem(low_tile + m, owners) ^ position
        chips, core = lax.div(apart, 2), lax.rem(apart, 2)
        part = slice(2 * (m // owners), 2 * (m // owners) + 2)
        pair = images[0][core, part, :]
        for i in range(1, owners // 2):
            other = 1 - core if partner_bits(i) % 2 else core
            pair = jnp.where(chips == i, images[i][other, part, :], pair)
        for w in range(2):
            img[MARGIN - 6 + 2 * m + w] = jnp.broadcast_to(pair[w : w + 1], (8, LANES))

    misfits = []
    new_b, old_b = b0, b1
    for t in range(STEPS):
        wide = 2 * reach - t
        for c in range(-wide, columns + wide):
            e = MARGIN + c
            b = img[e] * acc[t, e]
            if t > 0:
                (mid,), (laps,) = lap(new_b, e, 1, edges)
                b = b + 2.0 * mid + speed[e] * laps
            if t > 1:
                b = b - old_b[e]
            old_b[e] = b
        new_b, old_b = old_b, new_b
        misfits.append(
            {
                c: hit[reach + c] * new_b[MARGIN + c] + ahead[t, reach + c]
                for c in range(-t, columns + t)
            }
        )

    newer = older = None
    for t, q_t in zip(reversed(range(STEPS)), (q0, q1, q2, q3)):
        for c in range(-t, columns + t):
            e = MARGIN + c
            q = misfits[t][c]
            if newer is not None:
                (mid,), (laps,) = lap(newer, e, 1, edges)
                q = q + 2.0 * mid + speed[e] * laps
            if older is not None:
                q = q - older[e]
            q_t[e] = q
        newer, older = q_t, newer
    adjoint = (q3, q2, q1, q0)

    for k in range(tiles):
        owner = lax.rem(first + tiles * position + k, owners)
        for w in range(2):
            e = MARGIN + 2 * k + w
            part = slice(w * LANES, (w + 1) * LANES)
            grad = adjoint[0][e] * acc[0, e]
            for t in range(1, STEPS):
                grad = grad + adjoint[t][e] * acc[t, e]
            total = out[owner, :, part] + jnp.sum(grad, axis=0, keepdims=True)
            for group in range(groups):
                out[group * owners + owner, :, part] = total


def join_kernel(received, migrated, total, *, owners, groups):
    position = lax.axis_index("box")
    total[...] = jnp.zeros_like(total)
    for group in range(groups):
        start = received[group * owners, 0, 8 * LANES].astype(jnp.int32)
        base = lax.div(start - position + owners - 1, owners)
        for p in range(owners):
            total[base + p] = total[base + p] + received[group * owners + p, :, 0 : 8 * LANES]
    for r in range(migrated.shape[0]):
        grad = total[r, :, 0 : 4 * LANES]
        illum = total[r, :, 4 * LANES : 8 * LANES]
        image = grad / jnp.sqrt(illum + damping)
        for h in range(2):
            for w in range(2):
                i = 2 * h + w
                migrated[r, 0, w : w + 1, h * LANES : (h + 1) * LANES] = image[
                    :, i * LANES : (i + 1) * LANES
                ]


def on_device(
    u_prev,
    u_now,
    born_prev,
    born_now,
    adj_after,
    adj_last,
    velocity,
    wavelet,
    sources,
    receivers,
    observed,
    first_tile,
    reflectivity,
):
    owners = lax.axis_size("box")
    groups = lax.axis_size("shot")
    columns, depth = velocity.shape[1], velocity.shape[2]
    rounds = reflectivity.shape[0]
    vmem = pl.BlockSpec(memory_space=VMEM)
    anywhere = pl.BlockSpec(memory_space=pl.ANY)
    f32 = jnp.float32
    params = pltpu.CompilerParams(vmem_limit_bytes=24 * 1024 * 1024)
    params_hbm = pltpu.CompilerParams(vmem_limit_bytes=24 * 1024 * 1024)
    fields = (u_now, u_prev, born_now, born_prev, adj_last, adj_after)

    shape = jax.ShapeDtypeStruct
    blocks = 2 + pl.cdiv(receivers.shape[1], 8)
    pack_from = (sources, receivers, *fields, velocity, observed, reflectivity)
    send_a, send_b, info = pl.pallas_call(
        pack_kernel,
        out_shape=(
            VMEM((PACK_TILES + pl.cdiv(rounds, 4), 8, LANES), f32),
            VMEM((PACK_TILES, 8, LANES), f32),
            VMEM((blocks, 8, LANES), jnp.int32),
        ),
        in_specs=[anywhere] * 11,
        out_specs=(vmem,) * 3,
        scratch_shapes=[
            SMEM(sources.shape, jnp.int32),
            SMEM(receivers.shape, jnp.int32),
            VMEM(reflectivity.shape, f32),
            VMEM((2, 4, 8, 8, depth), f32),
            VMEM((2, 2, 8, 8, LANES), f32),
            VMEM((2, 8, depth), f32),
            VMEM(observed.shape, f32),
            pltpu.SemaphoreType.DMA((18,)),
        ],
        compiler_params=params_hbm,
        name="pack",
    )(*(pltpu.with_memory_space_constraint(x, pltpu.HBM) for x in pack_from))
    ends = (0, owners - 1)
    swap_a = [(i, i ^ 1) for i in range(owners)]
    swap_b = [
        (g * owners + i, (g ^ 1) * owners + i if i in ends else g * owners + (i + 1 if i % 2 else i - 1))
        for g in range(groups)
        for i in range(owners)
    ]
    got_a = lax.ppermute(send_a, "box", swap_a)
    got_b = lax.ppermute(send_b, ("shot", "box"), swap_b)
    info, *picks = pl.pallas_call(
        functools.partial(choose_kernel, columns=columns),
        out_shape=(VMEM((blocks, 8, LANES), jnp.int32),)
        + (VMEM((2, 4, LANES), f32),) * (owners // 2),
        in_specs=[pl.BlockSpec(memory_space=SMEM)] + [vmem] * 3,
        out_specs=(vmem,) * (1 + owners // 2),
        compiler_params=params,
        name="choose",
    )(first_tile, reflectivity, got_a, info)
    images = {0: picks[0]}
    for i in reversed(range(1, owners // 2)):
        pairs = [(j, j ^ partner_bits(i)) for j in range(owners)]
        images[i] = lax.ppermute(picks[i], "box", pairs)
    images = [images[i] for i in range(owners // 2)]

    ext = columns + 2 * MARGIN
    near = columns + 2 * (STEPS - 1)
    payload = shape((groups * owners, 1, 9 * LANES), f32)
    acc, near_speed, hit, ahead, part = pl.pallas_call(
        functools.partial(homogeneous_kernel, owners=owners, groups=groups),
        out_shape=(
            shape((STEPS, ext, 8, LANES), f32),
            shape((ext, 8, LANES), f32),
            shape((near, 8, LANES), f32),
            shape((STEPS, near, 8, LANES), f32),
            payload,
        ),
        in_specs=[vmem] * 12,
        out_specs=(vmem,) * 5,
        scratch_shapes=[VMEM((ext, 8, depth), f32)] * 2
        + [VMEM((ext, 8, LANES), f32)] * 2
        + [VMEM((ext, 8, depth), f32)] * 6
        + [VMEM((STEPS, columns, 8, LANES), f32), VMEM((2, 8, LANES), f32)],
        compiler_params=params,
        name="homogeneous",
    )(info, *fields, velocity, observed, wavelet, got_a, got_b)
    out = pl.pallas_call(
        functools.partial(scattered_kernel, owners=owners, groups=groups),
        out_shape=payload,
        in_specs=[vmem] * (6 + len(images)),
        out_specs=vmem,
        scratch_shapes=[VMEM((ext, 8, LANES), f32)] * 7,
        input_output_aliases={5 + len(images): 0},
        compiler_params=params,
        name="scattered",
    )(info, acc, near_speed, hit, ahead, *images, part)

    received = lax.all_to_all(out, ("shot", "box"), split_axis=0, concat_axis=0, tiled=True)
    return pl.pallas_call(
        functools.partial(join_kernel, owners=owners, groups=groups),
        out_shape=jax.ShapeDtypeStruct(reflectivity.shape, f32),
        in_specs=[vmem],
        out_specs=vmem,
        scratch_shapes=[VMEM((rounds, 1, 8 * LANES), f32)],
        compiler_params=params,
        name="join",
    )(received)


def solution(mesh):
    return jax.shard_map(
        on_device,
        mesh=mesh,
        in_specs=(
            P("shot", None, "box", None),
            P("shot", None, "box", None),
            P("shot", None, "box", None),
            P("shot", None, "box", None),
            P("shot", None, "box", None),
            P("shot", None, "box", None),
            P("shot", "box", None),
            P("shot", None, None),
            P("shot", None),
            P("shot", "box"),
            P("shot", None, None, "box"),
            P("shot"),
            P(None, "box", None, None),
        ),
        out_specs=P(None, "box", None, None),
        check_vma=False,
    )
```

```python
import functools

import jax
import jax.numpy as jnp
from jax import lax
from jax.experimental import pallas as pl
from jax.experimental.pallas import tpu as pltpu
from jax.sharding import PartitionSpec as P

damping = 1.0
LANES = 128
MARGIN = 8
STEPS = 4
HALO = (
    ("un", 0, 4),
    ("up", 0, 3),
    ("un", 1, 4),
    ("up", 1, 3),
    ("qn", 0, 4),
    ("qn", 1, 4),
    ("qp", 0, 3),
    ("qp", 1, 3),
)
NEAR = (
    *(("bn", j, j < 7) for j in range(1, 8)),
    *(("bp", j, j < 6) for j in range(1, 7)),
    *(("un", j, j < 7) for j in range(5, 8)),
    *(("up", j, j < 6) for j in range(4, 7)),
)
HALF = LANES // 2
MORE = 4
MORE_OF = [column for column in NEAR if column[2]]
NEAR_TILE = sum(count for _, _, count in HALO)
HALO_TILES = NEAR_TILE + (len(NEAR) + 1) // 2
SPEED_TILE = HALO_TILES
META_TILE = HALO_TILES + 2
PACK_TILES = HALO_TILES + 3
VMEM = pltpu.VMEM
SMEM = pltpu.SMEM


def partner_bits(i):
    return 2 * i + 1 if i else 0


def lane_iota():
    return lax.broadcasted_iota(jnp.int32, (8, LANES), 1)


def choose_kernel(first, own, pack_a, info_in, info, *picks, columns):
    info[...] = info_in[...]
    info[0] = jnp.full((8, LANES), first[0])
    start = first[0]
    position = lax.axis_index("box")
    owners = 2 * len(picks)
    rounds = own.shape[0]
    for i, pick in enumerate(picks):
        target = position ^ partner_bits(i)
        low_tile = start + (columns // 2) * target - 3
        for core in range(2):
            owner = position ^ core
            r0 = lax.div(low_tile - owner + 2 * owners - 1, owners) - 1
            for slot in range(2):
                r = jnp.clip(r0 + slot, 0, rounds - 1)
                if core == 0:
                    tile = own[r, 0, :, 0:LANES]
                else:
                    row = pl.multiple_of(2 * lax.rem(r, 4), 2)
                    tile = pack_a[PACK_TILES + lax.div(r, 4), pl.ds(row, 2), :]
                pick[core, 2 * slot : 2 * slot + 2, :] = tile


def pack_kernel(
    sources_any,
    rec_any,
    un_any,
    up_any,
    bn_any,
    bp_any,
    qn_any,
    qp_any,
    speed_any,
    obs_any,
    refl_any,
    pack_a,
    pack_b,
    info,
    un,
    up,
    bn,
    bp,
    qn,
    qp,
    speed,
    obs,
    refl,
    sources,
    rec,
    sems,
):
    columns, depth = un.shape[2], un.shape[3]
    position = lax.axis_index("box")
    even = lax.rem(position, 2) == 0
    lane = lane_iota()
    row = lax.broadcasted_iota(jnp.int32, (8, LANES), 0)
    fields = {"un": un, "up": up, "bn": bn, "bp": bp, "qn": qn, "qp": qp}

    small = ((sources_any, sources), (rec_any, rec), (obs_any, obs), (refl_any, refl))
    near = (slice(None),) * 3 + (pl.ds(0, LANES),)
    large = (
        (un_any, un),
        (up_any, up),
        (bn_any.at[near], bn),
        (bp_any.at[near], bp),
        (qn_any, qn),
        (qp_any, qp),
        (speed_any, speed),
    )
    copies = [
        pltpu.make_async_copy(*move, sems.at[i]) for i, move in enumerate(small + large)
    ]
    for copy in copies:
        copy.start()
    for copy in copies[: len(small)]:
        copy.wait()

    own_cell = position * columns * depth
    info[0] = jnp.zeros((8, LANES), jnp.int32)
    cell = jnp.zeros((8, LANES), jnp.int32)
    for s in range(8):
        cell = jnp.where(row == s, sources[0, s] - own_cell, cell)
    info[1] = cell
    count = rec.shape[1]
    edge_receivers = (0, 1, count - 1, count - 2)
    for block in range(0, count, 8):
        cell = jnp.zeros((8, LANES), jnp.int32)
        for r in range(min(8, count - block)):
            cell = jnp.where(row == r, rec[0, block + r] - own_cell, cell)
        info[2 + block // 8] = cell

    recorded = []
    for t in range(STEPS):
        at = obs[0, :, t, :]
        recorded.append([jnp.broadcast_to(at[:, r : r + 1], (8, LANES)) for r in edge_receivers])
    meta = []
    for side in range(2):
        out = jnp.zeros((8, LANES), jnp.float32)
        for k in range(2):
            r = edge_receivers[2 * side + k]
            for t in range(STEPS):
                out = jnp.where(lane == 2 * t + k, recorded[t][2 * side + k], out)
            column = lax.div(rec[0, r], depth) - position * columns
            distance = columns - column if side else column + 1
            code = distance * depth + lax.rem(rec[0, r], depth)
            out = jnp.where(lane == 2 * STEPS + k, code.astype(jnp.float32), out)
        meta.append(out)

    for r in range(refl.shape[0]):
        at = 2 * (r % 4)
        pack_a[PACK_TILES + r // 4, at : at + 2, :] = refl[r, 0, :, 0:LANES]
    for copy in copies[len(small) :]:
        copy.wait()

    def send(low_to, high_to):
        for side, to in ((0, low_to), (1, high_to)):
            if to is None:
                continue
            edge = slice(columns - 8, columns) if side else slice(0, 8)
            got = {}

            def column(name, half, j):
                if (name, half) not in got:
                    part = slice(half * LANES, (half + 1) * LANES)
                    got[name, half] = jnp.swapaxes(fields[name][0, :, edge, part], 0, 1)
                return got[name, half][8 - j if side else j - 1]

            tile = 0
            for name, half, width in HALO:
                for j in range(1, width + 1):
                    to[tile] = column(name, half, j)
                    tile += 1
            for i in range(0, len(NEAR), 2):
                out = column(NEAR[i][0], 0, NEAR[i][1])
                if i + 1 < len(NEAR):
                    other = column(NEAR[i + 1][0], 0, NEAR[i + 1][1])
                    out = jnp.where(lane < HALF, out, pltpu.roll(other, HALF, 1))
                else:
                    for k, (name, j, _) in enumerate(MORE_OF):
                        more = column(name, 0, j)
                        if k:
                            more = pltpu.roll(more, MORE * k, 1)
                        out = jnp.where(lane < HALF + MORE * k, out, more)
                to[tile] = out
                tile += 1
            for half in range(2):
                to[SPEED_TILE + half] = speed[0, edge, half * LANES : (half + 1) * LANES]
            to[META_TILE] = meta[side]

    is_end = jnp.logical_or(position == 0, position == lax.axis_size("box") - 1)

    @pl.when(jnp.logical_and(even, jnp.logical_not(is_end)))
    def _():
        send(pack_b, pack_a)

    @pl.when(jnp.logical_and(jnp.logical_not(even), jnp.logical_not(is_end)))
    def _():
        send(pack_a, pack_b)

    @pl.when(is_end)
    def _():
        pack_b[...] = jnp.zeros_like(pack_b)

    @pl.when(jnp.logical_and(even, is_end))
    def _():
        send(None, pack_a)

    @pl.when(jnp.logical_and(jnp.logical_not(even), is_end))
    def _():
        send(pack_a, None)


def depthwise(xs, first_lane, last_lane):
    rolled_up = [pltpu.roll(x, 1, 1) for x in xs]
    rolled_down = [pltpu.roll(x, LANES - 1, 1) for x in xs]
    if len(xs) == 1:
        return [
            jnp.where(first_lane, 0.0, rolled_up[0]) + jnp.where(last_lane, 0.0, rolled_down[0])
        ]
    return [
        jnp.where(first_lane, 0.0, rolled_up[0])
        + jnp.where(last_lane, rolled_down[1], rolled_down[0]),
        jnp.where(first_lane, rolled_up[0], rolled_up[1])
        + jnp.where(last_lane, 0.0, rolled_down[1]),
    ]


def lap(ref, e, count, edges):
    parts = [slice(h * LANES, (h + 1) * LANES) for h in range(count)]
    mid = [ref[e, :, part] for part in parts]
    along = depthwise(mid, *edges)
    return mid, [
        ref[e - 1, :, parts[h]] + ref[e + 1, :, parts[h]] + along[h] - 4.0 * mid[h]
        for h in range(count)
    ]


def homogeneous_kernel(
    info,
    un,
    up,
    bn,
    bp,
    qn,
    qp,
    speed,
    obs,
    wavelet,
    pack_a,
    pack_b,
    acc,
    near_speed,
    hit_out,
    ahead,
    out,
    u0,
    u1,
    b0,
    b1,
    q0,
    q1,
    q2,
    q3,
    q4,
    vel,
    late,
    metas,
    *,
    owners,
    groups,
):
    columns, depth = speed.shape[1], speed.shape[2]
    tiles = columns // 2
    position = lax.axis_index("box")
    even = lax.rem(position, 2) == 0
    lane = lane_iota()
    edges = lane == 0, lane == LANES - 1
    halves = (slice(0, LANES), slice(LANES, 2 * LANES))
    scratch = {"un": u0, "up": u1, "bn": b0, "bp": b1, "qn": q0, "qp": q1}
    first = info[0, 0, 0]

    for name, ref in (("un", un), ("up", up), ("qn", qn), ("qp", qp)):
        for c in range(0, columns, 8):
            scratch[name][MARGIN + c : MARGIN + c + 8] = jnp.swapaxes(ref[0, :, c : c + 8, :], 0, 1)
    for name, ref in (("bn", bn), ("bp", bp)):
        for c in range(0, columns, 8):
            scratch[name][MARGIN + c : MARGIN + c + 8] = jnp.swapaxes(
                ref[0, :, c : c + 8, :], 0, 1
            )
    for c in range(columns):
        vel[MARGIN + c] = jnp.broadcast_to(speed[0, c : c + 1, :], (8, depth))
        near_speed[MARGIN + c] = vel[MARGIN + c, :, halves[0]]

    def receive(left, right):
        for side, pack in ((0, left), (1, right)):

            def place(j):
                return MARGIN + columns - 1 + j if side else MARGIN - j

            tile = 0
            for name, half, count in HALO:
                for j in range(1, count + 1):
                    scratch[name][place(j), :, halves[half]] = pack[tile]
                    tile += 1
            more = pack[NEAR_TILE + len(NEAR) // 2]
            for i, column in enumerate(NEAR):
                name, j, needs_more = column
                value = pack[NEAR_TILE + i // 2]
                if i % 2:
                    value = pltpu.roll(value, HALF, 1)
                if needs_more:
                    k = MORE_OF.index(column)
                    rest = pltpu.roll(more, LANES - MORE * k, 1) if k else more
                    value = jnp.where(lane < HALF, value, rest)
                scratch[name][place(j), :, halves[0]] = value
        for half, count in ((0, 6), (1, 3)):
            for j in range(1, count + 1):
                for e, v in (
                    (MARGIN - j, left[SPEED_TILE + half, 8 - j : 9 - j, :]),
                    (MARGIN + columns - 1 + j, right[SPEED_TILE + half, j - 1 : j, :]),
                ):
                    v = jnp.broadcast_to(v, (8, LANES))
                    vel[e, :, halves[half]] = v
                    if half == 0:
                        near_speed[e] = v
        metas[0] = left[META_TILE]
        metas[1] = right[META_TILE]

    @pl.when(even)
    def _():
        receive(pack_b, pack_a)

    @pl.when(jnp.logical_not(even))
    def _():
        receive(pack_a, pack_b)

    meta = metas[0], metas[1]

    cell = info[1] - lane
    pulses = [jnp.broadcast_to(wavelet[0, :, t : t + 1], (8, LANES)) for t in range(STEPS)]
    new_u, old_u = u0, u1
    for t in range(STEPS):
        wide, narrow = 6 - t, 3 - t
        for c in range(-wide, columns + wide):
            e = MARGIN + c
            count = 2 if -narrow <= c < columns + narrow else 1
            mid, laps = lap(new_u, e, count, edges)
            for h in range(count):
                hit = cell == c * depth + h * LANES
                a = vel[e, :, halves[h]] * laps[h] + jnp.where(hit, pulses[t], 0.0)
                if h == 0:
                    acc[t, e] = a
                elif 0 <= c < columns:
                    late[t, c] = a
                if t < STEPS - 1:
                    old_u[e, :, halves[h]] = 2.0 * mid[h] - old_u[e, :, halves[h]] + a
        new_u, old_u = old_u, new_u

    reach = STEPS - 1
    recorded = {}
    own_obs = [obs[0, :, t, :] for t in range(STEPS)]
    for c in range(-reach, columns + reach):
        if 0 <= c < columns:
            r = c // 2
            here = jnp.broadcast_to(info[2 + r // 8, r % 8 : r % 8 + 1, :], (8, LANES))
            hit = lane == here - c * depth
            if c % 2 == 0:
                pair = [jnp.broadcast_to(at[:, r : r + 1], (8, LANES)) for at in own_obs]
            recorded[c] = pair
        else:
            j = -c if c < 0 else c - columns + 1
            side, k = meta[0] if c < 0 else meta[1], (j - 1) // 2
            code = jnp.broadcast_to(side[:, 2 * STEPS + k : 2 * STEPS + k + 1], (8, LANES))
            hit = code == (lane + j * depth).astype(jnp.float32)
            recorded[c] = [
                jnp.broadcast_to(side[:, 2 * t + k : 2 * t + k + 1], (8, LANES))
                for t in range(STEPS)
            ]
        hit_out[reach + c] = jnp.where(hit, 1.0, 0.0)
        for t in range(STEPS):
            if -t <= c < columns + t:
                ahead[t, reach + c] = recorded[c][t]
    new_b, old_b = b0, b1
    for t in range(STEPS):
        wide = 2 * reach - t
        for c in range(-wide, columns + wide):
            e = MARGIN + c
            (mid,), (laps,) = lap(new_b, e, 1, edges)
            b = 2.0 * mid - old_b[e] + vel[e, :, halves[0]] * laps
            if t < STEPS - 1:
                old_b[e] = b
            if -t <= c < columns + t:
                ahead[t, reach + c] = hit_out[reach + c] * (b - ahead[t, reach + c])
        new_b, old_b = old_b, new_b

    newer, older = q0, q1
    for t, q_t in zip(reversed(range(STEPS)), (q2, q3, q4, q1)):
        for c in range(-t, columns + t):
            e = MARGIN + c
            mid, laps = lap(newer, e, 2, edges)
            for h in range(2):
                q_t[e, :, halves[h]] = (
                    2.0 * mid[h] - older[e, :, halves[h]] + vel[e, :, halves[h]] * laps[h]
                )
        newer, older = q_t, newer
    adjoint = (q1, q4, q3, q2)

    start = jnp.full((1, LANES), first.astype(jnp.float32))
    for k in range(tiles):
        owner = lax.rem(first + tiles * position + k, owners)
        grads, illums = [], []
        for h in range(2):
            for w in range(2):
                c = 2 * k + w
                grad = illum = None
                for t in range(STEPS):
                    a = late[t, c] if h else acc[t, MARGIN + c]
                    g = adjoint[t][MARGIN + c, :, halves[h]] * a
                    grad = g if grad is None else grad + g
                    illum = a * a if illum is None else illum + a * a
                grads.append(grad)
                illums.append(illum)
        for i, total in enumerate(grads + illums):
            total = jnp.sum(total, axis=0, keepdims=True)
            for group in range(groups):
                out[group * owners + owner, :, i * LANES : (i + 1) * LANES] = total
        for group in range(groups):
            out[group * owners + owner, :, 8 * LANES : 9 * LANES] = start


def scattered_kernel(
    info,
    acc,
    speed,
    hit,
    ahead,
    *refs,
    owners,
    groups,
):
    images = refs[: owners // 2][::-1]
    _, out, b0, b1, q0, q1, q2, q3, img = refs[owners // 2 :]
    reach = STEPS - 1
    columns = hit.shape[0] - 2 * reach
    tiles = columns // 2
    position = lax.axis_index("box")
    lane = lane_iota()
    edges = lane == 0, lane == LANES - 1
    first = info[0, 0, 0]

    low_tile = first + tiles * position - 3 + owners
    for m in range(tiles + 6):
        apart = lax.rem(low_tile + m, owners) ^ position
        chips, core = lax.div(apart, 2), lax.rem(apart, 2)
        part = slice(2 * (m // owners), 2 * (m // owners) + 2)
        pair = images[0][core, part, :]
        for i in range(1, owners // 2):
            other = 1 - core if partner_bits(i) % 2 else core
            pair = jnp.where(chips == i, images[i][other, part, :], pair)
        for w in range(2):
            img[MARGIN - 6 + 2 * m + w] = jnp.broadcast_to(pair[w : w + 1], (8, LANES))

    misfits = []
    new_b, old_b = b0, b1
    for t in range(STEPS):
        wide = 2 * reach - t
        for c in range(-wide, columns + wide):
            e = MARGIN + c
            b = img[e] * acc[t, e]
            if t > 0:
                (mid,), (laps,) = lap(new_b, e, 1, edges)
                b = b + 2.0 * mid + speed[e] * laps
            if t > 1:
                b = b - old_b[e]
            old_b[e] = b
        new_b, old_b = old_b, new_b
        misfits.append(
            {
                c: hit[reach + c] * new_b[MARGIN + c] + ahead[t, reach + c]
                for c in range(-t, columns + t)
            }
        )

    newer = older = None
    for t, q_t in zip(reversed(range(STEPS)), (q0, q1, q2, q3)):
        for c in range(-t, columns + t):
            e = MARGIN + c
            q = misfits[t][c]
            if newer is not None:
                (mid,), (laps,) = lap(newer, e, 1, edges)
                q = q + 2.0 * mid + speed[e] * laps
            if older is not None:
                q = q - older[e]
            q_t[e] = q
        newer, older = q_t, newer
    adjoint = (q3, q2, q1, q0)

    for k in range(tiles):
        owner = lax.rem(first + tiles * position + k, owners)
        for w in range(2):
            e = MARGIN + 2 * k + w
            part = slice(w * LANES, (w + 1) * LANES)
            grad = adjoint[0][e] * acc[0, e]
            for t in range(1, STEPS):
                grad = grad + adjoint[t][e] * acc[t, e]
            total = out[owner, :, part] + jnp.sum(grad, axis=0, keepdims=True)
            for group in range(groups):
                out[group * owners + owner, :, part] = total


def join_kernel(received, migrated, total, *, owners, groups):
    position = lax.axis_index("box")
    total[...] = jnp.zeros_like(total)
    for group in range(groups):
        start = received[group * owners, 0, 8 * LANES].astype(jnp.int32)
        base = lax.div(start - position + owners - 1, owners)
        for p in range(owners):
            total[base + p] = total[base + p] + received[group * owners + p, :, 0 : 8 * LANES]
    for r in range(migrated.shape[0]):
        grad = total[r, :, 0 : 4 * LANES]
        illum = total[r, :, 4 * LANES : 8 * LANES]
        image = grad / jnp.sqrt(illum + damping)
        for h in range(2):
            for w in range(2):
                i = 2 * h + w
                migrated[r, 0, w : w + 1, h * LANES : (h + 1) * LANES] = image[
                    :, i * LANES : (i + 1) * LANES
                ]


def on_device(
    u_prev,
    u_now,
    born_prev,
    born_now,
    adj_after,
    adj_last,
    velocity,
    wavelet,
    sources,
    receivers,
    observed,
    first_tile,
    reflectivity,
):
    owners = lax.axis_size("box")
    groups = lax.axis_size("shot")
    columns, depth = velocity.shape[1], velocity.shape[2]
    rounds = reflectivity.shape[0]
    vmem = pl.BlockSpec(memory_space=VMEM)
    anywhere = pl.BlockSpec(memory_space=pl.ANY)
    f32 = jnp.float32
    params = pltpu.CompilerParams(vmem_limit_bytes=24 * 1024 * 1024)
    params_hbm = pltpu.CompilerParams(vmem_limit_bytes=24 * 1024 * 1024)
    fields = (u_now, u_prev, born_now, born_prev, adj_last, adj_after)

    shape = jax.ShapeDtypeStruct
    blocks = 2 + pl.cdiv(receivers.shape[1], 8)
    pack_from = (sources, receivers, *fields, velocity, observed, reflectivity)
    near_field = (*u_now.shape[:-1], LANES)
    kept = [near_field if i in (2, 3) else u_now.shape for i in range(6)]
    kept += [velocity.shape, observed.shape, reflectivity.shape]
    send_a, send_b, info, *kept = pl.pallas_call(
        pack_kernel,
        out_shape=(
            VMEM((PACK_TILES + pl.cdiv(rounds, 4), 8, LANES), f32),
            VMEM((PACK_TILES, 8, LANES), f32),
            VMEM((blocks, 8, LANES), jnp.int32),
            *(VMEM(dims, f32) for dims in kept),
        ),
        in_specs=[anywhere] * 11,
        out_specs=(vmem,) * 12,
        scratch_shapes=[
            SMEM(sources.shape, jnp.int32),
            SMEM(receivers.shape, jnp.int32),
            pltpu.SemaphoreType.DMA((11,)),
        ],
        compiler_params=params_hbm,
        name="pack",
    )(*(pltpu.with_memory_space_constraint(x, pltpu.HBM) for x in pack_from))
    *kept, own_tiles = kept

    ends = (0, owners - 1)
    swap_a = [(i, i ^ 1) for i in range(owners)]
    swap_b = [
        (g * owners + i, (g ^ 1) * owners + i if i in ends else g * owners + (i + 1 if i % 2 else i - 1))
        for g in range(groups)
        for i in range(owners)
    ]
    got_a = lax.ppermute(send_a, "box", swap_a)
    got_b = lax.ppermute(send_b, ("shot", "box"), swap_b)
    info, *picks = pl.pallas_call(
        functools.partial(choose_kernel, columns=columns),
        out_shape=(VMEM((blocks, 8, LANES), jnp.int32),)
        + (VMEM((2, 4, LANES), f32),) * (owners // 2),
        in_specs=[pl.BlockSpec(memory_space=SMEM)] + [vmem] * 3,
        out_specs=(vmem,) * (1 + owners // 2),
        compiler_params=params,
        name="choose",
    )(first_tile, own_tiles, got_a, info)
    images = {0: picks[0]}
    for i in reversed(range(1, owners // 2)):
        pairs = [(j, j ^ partner_bits(i)) for j in range(owners)]
        images[i] = lax.ppermute(picks[i], "box", pairs)
    images = [images[i] for i in reversed(range(owners // 2))]

    ext = columns + 2 * MARGIN
    near = columns + 2 * (STEPS - 1)
    payload = shape((groups * owners, 1, 9 * LANES), f32)
    acc, near_speed, hit, ahead, part = pl.pallas_call(
        functools.partial(homogeneous_kernel, owners=owners, groups=groups),
        out_shape=(
            shape((STEPS, ext, 8, LANES), f32),
            shape((ext, 8, LANES), f32),
            shape((near, 8, LANES), f32),
            shape((STEPS, near, 8, LANES), f32),
            payload,
        ),
        in_specs=[vmem] * 12,
        out_specs=(vmem,) * 5,
        scratch_shapes=[VMEM((ext, 8, depth), f32)] * 2
        + [VMEM((ext, 8, LANES), f32)] * 2
        + [VMEM((ext, 8, depth), f32)] * 6
        + [VMEM((STEPS, columns, 8, LANES), f32), VMEM((2, 8, LANES), f32)],
        compiler_params=params,
        name="homogeneous",
    )(info, *kept, wavelet, got_a, got_b)
    out = pl.pallas_call(
        functools.partial(scattered_kernel, owners=owners, groups=groups),
        out_shape=payload,
        in_specs=[vmem] * (6 + len(images)),
        out_specs=vmem,
        scratch_shapes=[VMEM((ext, 8, LANES), f32)] * 7,
        input_output_aliases={5 + len(images): 0},
        compiler_params=params,
        name="scattered",
    )(info, acc, near_speed, hit, ahead, *images, part)

    received = lax.all_to_all(out, ("shot", "box"), split_axis=0, concat_axis=0, tiled=True)
    return pl.pallas_call(
        functools.partial(join_kernel, owners=owners, groups=groups),
        out_shape=jax.ShapeDtypeStruct(reflectivity.shape, f32),
        in_specs=[vmem],
        out_specs=vmem,
        scratch_shapes=[VMEM((rounds, 1, 8 * LANES), f32)],
        compiler_params=params,
        name="join",
    )(received)


def solution(mesh):
    return jax.shard_map(
        on_device,
        mesh=mesh,
        in_specs=(
            P("shot", None, "box", None),
            P("shot", None, "box", None),
            P("shot", None, "box", None),
            P("shot", None, "box", None),
            P("shot", None, "box", None),
            P("shot", None, "box", None),
            P("shot", "box", None),
            P("shot", None, None),
            P("shot", None),
            P("shot", "box"),
            P("shot", None, None, "box"),
            P("shot"),
            P(None, "box", None, None),
        ),
        out_specs=P(None, "box", None, None),
        check_vma=False,
    )
```

```python
import functools

import jax
import jax.numpy as jnp
from jax import lax
from jax.experimental import pallas as pl
from jax.experimental.pallas import tpu as pltpu
from jax.sharding import PartitionSpec as P

damping = 1.0
LANES = 128
MARGIN = 8
STEPS = 4
HALO = (
    ("un", 0, 4),
    ("up", 0, 3),
    ("un", 1, 4),
    ("up", 1, 3),
    ("qn", 0, 4),
    ("qn", 1, 4),
    ("qp", 0, 3),
    ("qp", 1, 3),
)
NEAR = (
    *(("bn", j, j < 7) for j in range(1, 8)),
    *(("bp", j, j < 6) for j in range(1, 7)),
    *(("un", j, j < 7) for j in range(5, 8)),
    *(("up", j, j < 6) for j in range(4, 7)),
)
HALF = LANES // 2
MORE = 4
MORE_OF = [column for column in NEAR if column[2]]
NEAR_TILE = sum(count for _, _, count in HALO)
HALO_TILES = NEAR_TILE + (len(NEAR) + 1) // 2
SPEED_TILE = HALO_TILES
META_TILE = HALO_TILES + 2
PACK_TILES = HALO_TILES + 3
VMEM = pltpu.VMEM
SMEM = pltpu.SMEM


def partner_bits(i):
    return 2 * i + 1 if i else 0


def lane_iota():
    return lax.broadcasted_iota(jnp.int32, (8, LANES), 1)


def choose_kernel(first, own, pack_a, info_in, info, *picks, columns):
    info[...] = info_in[...]
    info[0] = jnp.full((8, LANES), first[0])
    start = first[0]
    position = lax.axis_index("box")
    owners = 2 * len(picks)
    rounds = own.shape[0]
    for i, pick in enumerate(picks):
        target = position ^ partner_bits(i)
        low_tile = start + (columns // 2) * target - 3
        for core in range(2):
            owner = position ^ core
            r0 = lax.div(low_tile - owner + 2 * owners - 1, owners) - 1
            for slot in range(2):
                r = jnp.clip(r0 + slot, 0, rounds - 1)
                if core == 0:
                    tile = own[r, 0, :, 0:LANES]
                else:
                    row = pl.multiple_of(2 * lax.rem(r, 4), 2)
                    tile = pack_a[PACK_TILES + lax.div(r, 4), pl.ds(row, 2), :]
                pick[core, 2 * slot : 2 * slot + 2, :] = tile


def pack_kernel(
    sources_any,
    rec_any,
    un_any,
    up_any,
    bn_any,
    bp_any,
    qn_any,
    qp_any,
    speed_any,
    obs_any,
    refl_any,
    pack_a,
    pack_b,
    info,
    un,
    up,
    bn,
    bp,
    qn,
    qp,
    speed,
    obs,
    refl,
    sources,
    rec,
    sems,
):
    columns, depth = un.shape[2], un.shape[3]
    position = lax.axis_index("box")
    even = lax.rem(position, 2) == 0
    lane = lane_iota()
    row = lax.broadcasted_iota(jnp.int32, (8, LANES), 0)
    fields = {"un": un, "up": up, "bn": bn, "bp": bp, "qn": qn, "qp": qp}

    small = ((sources_any, sources), (rec_any, rec), (obs_any, obs), (refl_any, refl))
    near = (slice(None),) * 3 + (pl.ds(0, LANES),)
    large = (
        (un_any, un),
        (up_any, up),
        (bn_any.at[near], bn),
        (bp_any.at[near], bp),
        (qn_any, qn),
        (qp_any, qp),
        (speed_any, speed),
    )
    copies = [
        pltpu.make_async_copy(*move, sems.at[i]) for i, move in enumerate(small + large)
    ]
    for copy in copies:
        copy.start()
    for copy in copies[: len(small)]:
        copy.wait()

    own_cell = position * columns * depth
    info[0] = jnp.zeros((8, LANES), jnp.int32)
    cell = jnp.zeros((8, LANES), jnp.int32)
    for s in range(8):
        cell = jnp.where(row == s, sources[0, s] - own_cell, cell)
    info[1] = cell
    count = rec.shape[1]
    edge_receivers = (0, 1, count - 1, count - 2)
    for block in range(0, count, 8):
        cell = jnp.zeros((8, LANES), jnp.int32)
        for r in range(min(8, count - block)):
            cell = jnp.where(row == r, rec[0, block + r] - own_cell, cell)
        info[2 + block // 8] = cell

    recorded = []
    for t in range(STEPS):
        at = obs[0, :, t, :]
        recorded.append([jnp.broadcast_to(at[:, r : r + 1], (8, LANES)) for r in edge_receivers])
    meta = []
    for side in range(2):
        out = jnp.zeros((8, LANES), jnp.float32)
        for k in range(2):
            r = edge_receivers[2 * side + k]
            for t in range(STEPS):
                out = jnp.where(lane == 2 * t + k, recorded[t][2 * side + k], out)
            column = lax.div(rec[0, r], depth) - position * columns
            distance = columns - column if side else column + 1
            code = distance * depth + lax.rem(rec[0, r], depth)
            out = jnp.where(lane == 2 * STEPS + k, code.astype(jnp.float32), out)
        meta.append(out)

    for r in range(refl.shape[0]):
        at = 2 * (r % 4)
        pack_a[PACK_TILES + r // 4, at : at + 2, :] = refl[r, 0, :, 0:LANES]
    for copy in copies[len(small) :]:
        copy.wait()

    def send(low_to, high_to):
        for side, to in ((0, low_to), (1, high_to)):
            if to is None:
                continue
            edge = slice(columns - 8, columns) if side else slice(0, 8)
            got = {}

            def column(name, half, j):
                if (name, half) not in got:
                    part = slice(half * LANES, (half + 1) * LANES)
                    got[name, half] = jnp.swapaxes(fields[name][0, :, edge, part], 0, 1)
                return got[name, half][8 - j if side else j - 1]

            tile = 0
            for name, half, width in HALO:
                for j in range(1, width + 1):
                    to[tile] = column(name, half, j)
                    tile += 1
            for i in range(0, len(NEAR), 2):
                out = column(NEAR[i][0], 0, NEAR[i][1])
                if i + 1 < len(NEAR):
                    other = column(NEAR[i + 1][0], 0, NEAR[i + 1][1])
                    out = jnp.where(lane < HALF, out, pltpu.roll(other, HALF, 1))
                else:
                    for k, (name, j, _) in enumerate(MORE_OF):
                        more = column(name, 0, j)
                        if k:
                            more = pltpu.roll(more, MORE * k, 1)
                        out = jnp.where(lane < HALF + MORE * k, out, more)
                to[tile] = out
                tile += 1
            for half in range(2):
                to[SPEED_TILE + half] = speed[0, edge, half * LANES : (half + 1) * LANES]
            to[META_TILE] = meta[side]

    is_end = jnp.logical_or(position == 0, position == lax.axis_size("box") - 1)

    @pl.when(jnp.logical_and(even, jnp.logical_not(is_end)))
    def _():
        send(pack_b, pack_a)

    @pl.when(jnp.logical_and(jnp.logical_not(even), jnp.logical_not(is_end)))
    def _():
        send(pack_a, pack_b)

    @pl.when(is_end)
    def _():
        pack_b[...] = jnp.zeros_like(pack_b)

    @pl.when(jnp.logical_and(even, is_end))
    def _():
        send(None, pack_a)

    @pl.when(jnp.logical_and(jnp.logical_not(even), is_end))
    def _():
        send(pack_a, None)


def depthwise(xs, first_lane, last_lane):
    rolled_up = [pltpu.roll(x, 1, 1) for x in xs]
    rolled_down = [pltpu.roll(x, LANES - 1, 1) for x in xs]
    if len(xs) == 1:
        return [
            jnp.where(first_lane, 0.0, rolled_up[0]) + jnp.where(last_lane, 0.0, rolled_down[0])
        ]
    return [
        jnp.where(first_lane, 0.0, rolled_up[0])
        + jnp.where(last_lane, rolled_down[1], rolled_down[0]),
        jnp.where(first_lane, rolled_up[0], rolled_up[1])
        + jnp.where(last_lane, 0.0, rolled_down[1]),
    ]


def lap(ref, e, count, edges):
    parts = [slice(h * LANES, (h + 1) * LANES) for h in range(count)]
    mid = [ref[e, :, part] for part in parts]
    along = depthwise(mid, *edges)
    return mid, [
        ref[e - 1, :, parts[h]] + ref[e + 1, :, parts[h]] + along[h] - 4.0 * mid[h]
        for h in range(count)
    ]


def homogeneous_kernel(
    info,
    un,
    up,
    bn,
    bp,
    qn,
    qp,
    speed,
    obs,
    wavelet,
    pack_a,
    pack_b,
    acc,
    near_speed,
    hit_out,
    ahead,
    out,
    u0,
    u1,
    b0,
    b1,
    q0,
    q1,
    q2,
    q3,
    q4,
    vel,
    late,
    metas,
    *,
    owners,
    groups,
):
    columns, depth = speed.shape[1], speed.shape[2]
    tiles = columns // 2
    position = lax.axis_index("box")
    even = lax.rem(position, 2) == 0
    lane = lane_iota()
    edges = lane == 0, lane == LANES - 1
    halves = (slice(0, LANES), slice(LANES, 2 * LANES))
    scratch = {"un": u0, "up": u1, "bn": b0, "bp": b1, "qn": q0, "qp": q1}
    first = info[0, 0, 0]

    for name, ref in (("un", un), ("up", up), ("qn", qn), ("qp", qp)):
        for c in range(0, columns, 8):
            scratch[name][MARGIN + c : MARGIN + c + 8] = jnp.swapaxes(ref[0, :, c : c + 8, :], 0, 1)
    for name, ref in (("bn", bn), ("bp", bp)):
        for c in range(0, columns, 8):
            scratch[name][MARGIN + c : MARGIN + c + 8] = jnp.swapaxes(
                ref[0, :, c : c + 8, :], 0, 1
            )
    for c in range(columns):
        vel[MARGIN + c] = jnp.broadcast_to(speed[0, c : c + 1, :], (8, depth))
        near_speed[MARGIN + c] = vel[MARGIN + c, :, halves[0]]

    def receive(left, right):
        for side, pack in ((0, left), (1, right)):

            def place(j):
                return MARGIN + columns - 1 + j if side else MARGIN - j

            tile = 0
            for name, half, count in HALO:
                for j in range(1, count + 1):
                    scratch[name][place(j), :, halves[half]] = pack[tile]
                    tile += 1
            more = pack[NEAR_TILE + len(NEAR) // 2]
            for i, column in enumerate(NEAR):
                name, j, needs_more = column
                value = pack[NEAR_TILE + i // 2]
                if i % 2:
                    value = pltpu.roll(value, HALF, 1)
                if needs_more:
                    k = MORE_OF.index(column)
                    rest = pltpu.roll(more, LANES - MORE * k, 1) if k else more
                    value = jnp.where(lane < HALF, value, rest)
                scratch[name][place(j), :, halves[0]] = value
        for half, count in ((0, 6), (1, 3)):
            for j in range(1, count + 1):
                for e, v in (
                    (MARGIN - j, left[SPEED_TILE + half, 8 - j : 9 - j, :]),
                    (MARGIN + columns - 1 + j, right[SPEED_TILE + half, j - 1 : j, :]),
                ):
                    v = jnp.broadcast_to(v, (8, LANES))
                    vel[e, :, halves[half]] = v
                    if half == 0:
                        near_speed[e] = v
        metas[0] = left[META_TILE]
        metas[1] = right[META_TILE]

    @pl.when(even)
    def _():
        receive(pack_b, pack_a)

    @pl.when(jnp.logical_not(even))
    def _():
        receive(pack_a, pack_b)

    meta = metas[0], metas[1]

    cell = info[1] - lane
    pulses = [jnp.broadcast_to(wavelet[0, :, t : t + 1], (8, LANES)) for t in range(STEPS)]
    new_u, old_u = u0, u1
    for t in range(STEPS):
        wide, narrow = 6 - t, 3 - t
        for c in range(-wide, columns + wide):
            e = MARGIN + c
            count = 2 if -narrow <= c < columns + narrow else 1
            mid, laps = lap(new_u, e, count, edges)
            for h in range(count):
                hit = cell == c * depth + h * LANES
                a = vel[e, :, halves[h]] * laps[h] + jnp.where(hit, pulses[t], 0.0)
                if h == 0:
                    acc[t, e] = a
                elif 0 <= c < columns:
                    late[t, c] = a
                if t < STEPS - 1:
                    old_u[e, :, halves[h]] = 2.0 * mid[h] - old_u[e, :, halves[h]] + a
        new_u, old_u = old_u, new_u

    reach = STEPS - 1
    recorded = {}
    own_obs = [obs[0, :, t, :] for t in range(STEPS)]
    for c in range(-reach, columns + reach):
        if 0 <= c < columns:
            r = c // 2
            here = jnp.broadcast_to(info[2 + r // 8, r % 8 : r % 8 + 1, :], (8, LANES))
            hit = lane == here - c * depth
            if c % 2 == 0:
                pair = [jnp.broadcast_to(at[:, r : r + 1], (8, LANES)) for at in own_obs]
            recorded[c] = pair
        else:
            j = -c if c < 0 else c - columns + 1
            side, k = meta[0] if c < 0 else meta[1], (j - 1) // 2
            code = jnp.broadcast_to(side[:, 2 * STEPS + k : 2 * STEPS + k + 1], (8, LANES))
            hit = code == (lane + j * depth).astype(jnp.float32)
            recorded[c] = [
                jnp.broadcast_to(side[:, 2 * t + k : 2 * t + k + 1], (8, LANES))
                for t in range(STEPS)
            ]
        hit_out[reach + c] = jnp.where(hit, 1.0, 0.0)
        for t in range(STEPS):
            if -t <= c < columns + t:
                ahead[t, reach + c] = recorded[c][t]
    new_b, old_b = b0, b1
    for t in range(STEPS):
        wide = 2 * reach - t
        for c in range(-wide, columns + wide):
            e = MARGIN + c
            (mid,), (laps,) = lap(new_b, e, 1, edges)
            b = 2.0 * mid - old_b[e] + vel[e, :, halves[0]] * laps
            if t < STEPS - 1:
                old_b[e] = b
            if -t <= c < columns + t:
                ahead[t, reach + c] = hit_out[reach + c] * (b - ahead[t, reach + c])
        new_b, old_b = old_b, new_b

    newer, older = q0, q1
    for t, q_t in zip(reversed(range(STEPS)), (q2, q3, q4, q1)):
        for c in range(-t, columns + t):
            e = MARGIN + c
            mid, laps = lap(newer, e, 2, edges)
            for h in range(2):
                q_t[e, :, halves[h]] = (
                    2.0 * mid[h] - older[e, :, halves[h]] + vel[e, :, halves[h]] * laps[h]
                )
        newer, older = q_t, newer
    adjoint = (q1, q4, q3, q2)

    start = jnp.full((1, LANES), first.astype(jnp.float32))
    for k in range(tiles):
        owner = lax.rem(first + tiles * position + k, owners)
        grads, illums = [], []
        for h in range(2):
            for w in range(2):
                c = 2 * k + w
                grad = illum = None
                for t in range(STEPS):
                    a = late[t, c] if h else acc[t, MARGIN + c]
                    g = adjoint[t][MARGIN + c, :, halves[h]] * a
                    grad = g if grad is None else grad + g
                    illum = a * a if illum is None else illum + a * a
                grads.append(grad)
                illums.append(illum)
        for i, total in enumerate(grads + illums):
            total = jnp.sum(total, axis=0, keepdims=True)
            for group in range(groups):
                out[group * owners + owner, :, i * LANES : (i + 1) * LANES] = total
        for group in range(groups):
            out[group * owners + owner, :, 8 * LANES : 9 * LANES] = start


def scattered_kernel(
    info,
    acc,
    speed,
    hit,
    ahead,
    *refs,
    owners,
    groups,
):
    images = refs[: owners // 2][::-1]
    _, out, b0, b1, q0, q1, q2, q3, img = refs[owners // 2 :]
    reach = STEPS - 1
    columns = hit.shape[0] - 2 * reach
    tiles = columns // 2
    position = lax.axis_index("box")
    lane = lane_iota()
    edges = lane == 0, lane == LANES - 1
    first = info[0, 0, 0]

    low_tile = first + tiles * position - 3 + owners
    for m in range(tiles + 6):
        apart = ((low_tile + m) & (owners - 1)) ^ position
        chips, core = apart >> 1, apart & 1
        part = slice(2 * (m // owners), 2 * (m // owners) + 2)
        pair = images[0][core, part, :]
        for i in range(1, owners // 2):
            other = 1 - core if partner_bits(i) % 2 else core
            pair = jnp.where(chips == i, images[i][other, part, :], pair)
        for w in range(2):
            img[MARGIN - 6 + 2 * m + w] = jnp.broadcast_to(pair[w : w + 1], (8, LANES))

    misfits = []
    new_b, old_b = b0, b1
    for t in range(STEPS):
        wide = 2 * reach - t
        for c in range(-wide, columns + wide):
            e = MARGIN + c
            b = img[e] * acc[t, e]
            if t > 0:
                (mid,), (laps,) = lap(new_b, e, 1, edges)
                b = b + 2.0 * mid + speed[e] * laps
            if t > 1:
                b = b - old_b[e]
            old_b[e] = b
        new_b, old_b = old_b, new_b
        misfits.append(
            {
                c: hit[reach + c] * new_b[MARGIN + c] + ahead[t, reach + c]
                for c in range(-t, columns + t)
            }
        )

    newer = older = None
    for t, q_t in zip(reversed(range(STEPS)), (q0, q1, q2, q3)):
        for c in range(-t, columns + t):
            e = MARGIN + c
            q = misfits[t][c]
            if newer is not None:
                (mid,), (laps,) = lap(newer, e, 1, edges)
                q = q + 2.0 * mid + speed[e] * laps
            if older is not None:
                q = q - older[e]
            q_t[e] = q
        newer, older = q_t, newer
    adjoint = (q3, q2, q1, q0)

    for k in range(tiles):
        owner = (first + tiles * position + k) & (owners - 1)
        for w in range(2):
            e = MARGIN + 2 * k + w
            part = slice(w * LANES, (w + 1) * LANES)
            grad = adjoint[0][e] * acc[0, e]
            for t in range(1, STEPS):
                grad = grad + adjoint[t][e] * acc[t, e]
            total = out[owner, :, part] + jnp.sum(grad, axis=0, keepdims=True)
            for group in range(groups):
                out[group * owners + owner, :, part] = total


def join_kernel(received, migrated, total, *, owners, groups):
    position = lax.axis_index("box")
    total[...] = jnp.zeros_like(total)
    for group in range(groups):
        start = received[group * owners, 0, 8 * LANES].astype(jnp.int32)
        base = lax.div(start - position + owners - 1, owners)
        for p in range(owners):
            total[base + p] = total[base + p] + received[group * owners + p, :, 0 : 8 * LANES]
    for r in range(migrated.shape[0]):
        grad = total[r, :, 0 : 4 * LANES]
        illum = total[r, :, 4 * LANES : 8 * LANES]
        image = grad / jnp.sqrt(illum + damping)
        for h in range(2):
            for w in range(2):
                i = 2 * h + w
                migrated[r, 0, w : w + 1, h * LANES : (h + 1) * LANES] = image[
                    :, i * LANES : (i + 1) * LANES
                ]


def on_device(
    u_prev,
    u_now,
    born_prev,
    born_now,
    adj_after,
    adj_last,
    velocity,
    wavelet,
    sources,
    receivers,
    observed,
    first_tile,
    reflectivity,
):
    owners = lax.axis_size("box")
    groups = lax.axis_size("shot")
    columns, depth = velocity.shape[1], velocity.shape[2]
    rounds = reflectivity.shape[0]
    vmem = pl.BlockSpec(memory_space=VMEM)
    anywhere = pl.BlockSpec(memory_space=pl.ANY)
    f32 = jnp.float32
    params = pltpu.CompilerParams(vmem_limit_bytes=24 * 1024 * 1024)
    params_hbm = pltpu.CompilerParams(vmem_limit_bytes=24 * 1024 * 1024)
    fields = (u_now, u_prev, born_now, born_prev, adj_last, adj_after)

    shape = jax.ShapeDtypeStruct
    blocks = 2 + pl.cdiv(receivers.shape[1], 8)
    pack_from = (sources, receivers, *fields, velocity, observed, reflectivity)
    near_field = (*u_now.shape[:-1], LANES)
    kept = [near_field if i in (2, 3) else u_now.shape for i in range(6)]
    kept += [velocity.shape, observed.shape, reflectivity.shape]
    send_a, send_b, info, *kept = pl.pallas_call(
        pack_kernel,
        out_shape=(
            VMEM((PACK_TILES + pl.cdiv(rounds, 4), 8, LANES), f32),
            VMEM((PACK_TILES, 8, LANES), f32),
            VMEM((blocks, 8, LANES), jnp.int32),
            *(VMEM(dims, f32) for dims in kept),
        ),
        in_specs=[anywhere] * 11,
        out_specs=(vmem,) * 12,
        scratch_shapes=[
            SMEM(sources.shape, jnp.int32),
            SMEM(receivers.shape, jnp.int32),
            pltpu.SemaphoreType.DMA((11,)),
        ],
        compiler_params=params_hbm,
        name="pack",
    )(*(pltpu.with_memory_space_constraint(x, pltpu.HBM) for x in pack_from))
    *kept, own_tiles = kept

    ends = (0, owners - 1)
    swap_a = [(i, i ^ 1) for i in range(owners)]
    swap_b = [
        (g * owners + i, (g ^ 1) * owners + i if i in ends else g * owners + (i + 1 if i % 2 else i - 1))
        for g in range(groups)
        for i in range(owners)
    ]
    got_a = lax.ppermute(send_a, "box", swap_a)
    got_b = lax.ppermute(send_b, ("shot", "box"), swap_b)
    info, *picks = pl.pallas_call(
        functools.partial(choose_kernel, columns=columns),
        out_shape=(VMEM((blocks, 8, LANES), jnp.int32),)
        + (VMEM((2, 4, LANES), f32),) * (owners // 2),
        in_specs=[pl.BlockSpec(memory_space=SMEM)] + [vmem] * 3,
        out_specs=(vmem,) * (1 + owners // 2),
        compiler_params=params,
        name="choose",
    )(first_tile, own_tiles, got_a, info)
    images = {0: picks[0]}
    for i in reversed(range(1, owners // 2)):
        pairs = [(j, j ^ partner_bits(i)) for j in range(owners)]
        images[i] = lax.ppermute(picks[i], "box", pairs)
    images = [images[i] for i in reversed(range(owners // 2))]

    ext = columns + 2 * MARGIN
    near = columns + 2 * (STEPS - 1)
    payload = shape((groups * owners, 1, 9 * LANES), f32)
    acc, near_speed, hit, ahead, part = pl.pallas_call(
        functools.partial(homogeneous_kernel, owners=owners, groups=groups),
        out_shape=(
            shape((STEPS, ext, 8, LANES), f32),
            shape((ext, 8, LANES), f32),
            shape((near, 8, LANES), f32),
            shape((STEPS, near, 8, LANES), f32),
            payload,
        ),
        in_specs=[vmem] * 12,
        out_specs=(vmem,) * 5,
        scratch_shapes=[VMEM((ext, 8, depth), f32)] * 2
        + [VMEM((ext, 8, LANES), f32)] * 2
        + [VMEM((ext, 8, depth), f32)] * 6
        + [VMEM((STEPS, columns, 8, LANES), f32), VMEM((2, 8, LANES), f32)],
        compiler_params=params,
        name="homogeneous",
    )(info, *kept, wavelet, got_a, got_b)
    out = pl.pallas_call(
        functools.partial(scattered_kernel, owners=owners, groups=groups),
        out_shape=payload,
        in_specs=[vmem] * (6 + len(images)),
        out_specs=vmem,
        scratch_shapes=[VMEM((ext, 8, LANES), f32)] * 7,
        input_output_aliases={5 + len(images): 0},
        compiler_params=params,
        name="scattered",
    )(info, acc, near_speed, hit, ahead, *images, part)

    received = lax.all_to_all(out, ("shot", "box"), split_axis=0, concat_axis=0, tiled=True)
    return pl.pallas_call(
        functools.partial(join_kernel, owners=owners, groups=groups),
        out_shape=jax.ShapeDtypeStruct(reflectivity.shape, f32),
        in_specs=[vmem],
        out_specs=vmem,
        scratch_shapes=[VMEM((rounds, 1, 8 * LANES), f32)],
        compiler_params=params,
        name="join",
    )(received)


def solution(mesh):
    return jax.shard_map(
        on_device,
        mesh=mesh,
        in_specs=(
            P("shot", None, "box", None),
            P("shot", None, "box", None),
            P("shot", None, "box", None),
            P("shot", None, "box", None),
            P("shot", None, "box", None),
            P("shot", None, "box", None),
            P("shot", "box", None),
            P("shot", None, None),
            P("shot", None),
            P("shot", "box"),
            P("shot", None, None, "box"),
            P("shot"),
            P(None, "box", None, None),
        ),
        out_specs=P(None, "box", None, None),
        check_vma=False,
    )
```
